512 devices in a mesh: seq: 16 (over y, core), exp: 8 (over z), ffn: 4 (over x).
Axes of the slice: x: 4, y: 8, z: 8, core: 2. Of those that a mesh axis runs over, the one named last changes fastest.
Arguments:
- tokens: bfloat16 [4096, 2048], P('seq', 'ffn'), may hold values from -6 to 6
- out_grad: bfloat16 [4096, 2048], P('seq', 'ffn'), may hold values from -6 to 6
- gate_prob: bfloat16 [4096, 2], P('seq'), may hold values from 0.049804688 to 0.94921875
- routing: int32 [4096, 2], P('seq'), may hold values from 0 to 15, all different within a row; in each aligned block of 256 rows (0 to 255, 256 to 511, ...) at most 48 rows name the same one
- weight_in: bfloat16 [16, 2048, 8192], P('exp', 'ffn', 'seq'), may hold values from -0.125 to 0.125
- weight_out: bfloat16 [16, 8192, 2048], P('exp', 'seq', 'ffn'), may hold values from -0.0625 to 0.0625
Outputs:
- grad_tokens: bfloat16 [4096, 2048], P(('seq', 'exp'), 'ffn')
- grad_gate: float32 [4096, 2], P(('seq', 'exp'))
- grad_weight_in: bfloat16 [16, 2048, 8192], P('exp', 'ffn', 'seq')
- grad_weight_out: bfloat16 [16, 8192, 2048], P('exp', 'seq', 'ffn')
The draws below stay inside these ranges and needn't reach their ends.
Inputs may be any that keep to these rules, and one draw needn't show every extreme that they name: `routing`: within the 256 rows of one token group no expert is named more than 48 times, and in every draw some expert is named exactly 48 times in some group; the 2 ids of a row differ, and every expert is named somewhere.
All inputs are finite; a program needn't handle non-finite values.
Results may differ from the reference program's by a relative error of at most 0.029.
Values may be sent and summed in bfloat16 or wider, within the bound.
A program may use at most 64 MiB of HBM per device.

```python
import math
import jax
import jax.numpy as jnp
import numpy as np
from jax import lax

D = 2048
FF = 8192
TOP = 2
TOK_DEV = 256
EXPERTS = 16
CAP_SRC = 48
TOKENS = 4096
N_SEQ = 16
N_FFN = 4


def block_levels(own_key, dims, cuts, smallest, top_value):
    level, own = 1.0, jax.random.fold_in(own_key, 6)
    for axis_at, shards_of in cuts:
        heights = jnp.exp(jax.random.uniform(jax.random.fold_in(own, axis_at), (shards_of,), jnp.float32, smallest / len(cuts), top_value / len(cuts)))
        level = level * jnp.repeat(heights, dims[axis_at] // shards_of).reshape([-1 if axis == axis_at else 1 for axis in range(len(dims))])
    return level


def deal_out(rng, own, number, rows, amount, top, bound, slope):
    ranking = jax.random.permutation(rng, amount)
    heavy_load, ordinary = load_shares(amount, rows * top, bound, slope, True), load_shares(amount, rows * top, bound, slope, False)
    places = jnp.arange(amount)

    def named(tallies, offset_by):
        used = int((tallies > 0).sum())
        fixed = max(1, used // 4)
        shifted = fixed + (places - fixed + offset_by * (used - fixed)) % max(1, amount - fixed)
        return jnp.zeros((amount,), jnp.int32).at[ranking[jnp.where(places < fixed, places, shifted)]].set(jnp.asarray(tallies, jnp.int32))

    tallies = jnp.where(number % 4 == 0, named(heavy_load, number // 4), named(ordinary, number - number // 4 - 1))
    mixed = jax.random.permutation(jax.random.fold_in(own, 3), amount)
    giver, receiver = mixed[0:amount // 2 * 2:2], mixed[1:amount // 2 * 2:2]
    room = jnp.minimum(tallies[giver] - 1, bound - tallies[receiver]) // 2
    room = jnp.where((giver == ranking[0]) | (receiver == ranking[0]) | (tallies[receiver] == 0), 0, jnp.maximum(room, 0))
    shifted = jax.random.randint(jax.random.fold_in(own, 4), (amount // 2,), 0, 1 << 20) % (room + 1)
    tallies = tallies.at[giver].add(-shifted).at[receiver].add(shifted)
    items = jnp.searchsorted(jnp.cumsum(tallies), jnp.arange(rows * top), side="right").astype(jnp.int32)
    grid = items.reshape(top, rows).T
    grid = grid[jax.random.permutation(jax.random.fold_in(own, 1), rows)]
    offset_by = jax.random.randint(jax.random.fold_in(own, 2), (rows, 1), 0, top)
    return jnp.take_along_axis(grid, (jnp.arange(top)[None, :] + offset_by) % top, axis=1)


def load_shares(count, total, most, skew, full):
    portions = [(1 << 20) // math.isqrt(rank ** skew) + 1 for rank in range(1, count + 1)]
    largest = most if full else min(most, max(-(-total // count), total * portions[0] // sum(portions)))
    least = 1 if total - largest >= count - 1 else 0
    holding, rest = [largest] + [least] * (count - 1), total - largest - least * (count - 1)
    while rest > 0:
        free = [i for i in range(1, count) if holding[i] < largest] or [i for i in range(1, count) if holding[i] < most]
        pool, left = sum([portions[i] for i in free]), rest
        for i in free:
            addition = min(most - holding[i], max(1, left * portions[i] // pool), rest)
            holding[i] = holding[i] + addition
            rest = rest - addition
    return np.array(holding)


def scatter_about(rng, extent, width, bound, split=(), held_as=jnp.bfloat16):
    factor_of = block_levels(rng, extent, split, -0.22, 0.18) if split else 1.0
    values = jax.random.normal(rng, extent, jnp.float32) * width * factor_of
    return jnp.minimum(jnp.maximum(values, -bound), bound).astype(held_as)


def setup_inputs(seed: int = 0) -> dict:
    arg_keys = jax.random.split(jax.random.key(seed), 7)
    tokens = scatter_about(arg_keys[0], (TOKENS, D), 1.0, 6.0, ((0, 16), (1, 4)))
    out_grad = scatter_about(arg_keys[1], (TOKENS, D), 1.0, 6.0, ((0, 16), (1, 4)))
    gate_prob = jnp.clip(0.049804688 + 0.89941406 * jax.random.uniform(arg_keys[2], (TOKENS, TOP), jnp.float32) ** block_levels(arg_keys[2], (TOKENS, TOP), ((0, 16),), -0.2, 0.2), 0.049804688, 0.94921875).astype(jnp.bfloat16)
    routing_keys = jax.random.split(jax.random.fold_in(arg_keys[3], 1), TOKENS // TOK_DEV)
    routing_turns = jax.random.permutation(jax.random.fold_in(arg_keys[3], 3), TOKENS // TOK_DEV)
    routing = jax.vmap(lambda own, number: deal_out(jax.random.fold_in(arg_keys[3], 2), own, number, TOK_DEV, EXPERTS, TOP, CAP_SRC, 2))(routing_keys, routing_turns).reshape((TOKENS, TOP))
    weight_in = scatter_about(arg_keys[4], (EXPERTS, D, FF), D ** -0.5, 0.125, ((0, 8), (1, 4), (2, 16)))
    weight_out = scatter_about(arg_keys[5], (EXPERTS, FF, D), FF ** -0.5, 0.0625, ((0, 8), (1, 16), (2, 4)))
    return {"tokens": tokens, "out_grad": out_grad, "gate_prob": gate_prob, "routing": routing, "weight_in": weight_in, "weight_out": weight_out}


gelu_scale = 0.7978845608028654
gelu_cubic = 0.044715


def gelu_parts(pre_act):
    inner_arg = gelu_scale * (pre_act + gelu_cubic * pre_act * pre_act * pre_act)
    tangent = jnp.tanh(inner_arg)
    activated = 0.5 * pre_act * (1.0 + tangent)
    slope_value = 0.5 * (1.0 + tangent) + 0.5 * pre_act * (1.0 - tangent * tangent) * gelu_scale * (1.0 + 3.0 * gelu_cubic * pre_act * pre_act)
    return activated, slope_value


def slot_table(routing):
    chosen_flat = routing.reshape(N_SEQ, TOK_DEV * TOP)
    expert_ids = jnp.arange(EXPERTS, dtype=jnp.int32)
    hit_table = (chosen_flat[:, :, None] == expert_ids[None, None, :]).astype(jnp.int32)
    before = jnp.cumsum(hit_table, axis=1) - hit_table
    position = jnp.sum(hit_table * before, axis=2)
    source = jnp.arange(N_SEQ, dtype=jnp.int32)[:, None]
    slots = (source * CAP_SRC + position).reshape(-1).astype(jnp.int32)
    return chosen_flat.reshape(-1).astype(jnp.int32), slots


def expert_backward(operands):
    slot_x, slot_y, slot_gate, weight_in, weight_out = operands
    block_width = D // N_FFN
    slot_count = slot_x.shape[0]
    hidden = jnp.zeros((slot_count, FF), jnp.float32)
    upper_sum = jnp.zeros((slot_count, FF), jnp.float32)
    for ffn_block in range(N_FFN):
        offset = ffn_block * block_width
        partial_value = jnp.dot(slot_x[:, offset:offset + block_width], weight_in[offset:offset + block_width, :], preferred_element_type=jnp.float32)
        hidden = hidden + lax.optimization_barrier(partial_value.astype(jnp.bfloat16)).astype(jnp.float32)
        partial_value = jnp.dot(slot_y[:, offset:offset + block_width], weight_out[:, offset:offset + block_width].T, preferred_element_type=jnp.float32)
        upper_sum = upper_sum + lax.optimization_barrier(partial_value.astype(jnp.bfloat16)).astype(jnp.float32)
    activated, slope_value = gelu_parts(hidden)
    gate_column = slot_gate.astype(jnp.float32)[:, None]
    active = activated.astype(jnp.bfloat16)
    delta_rows = (gate_column * upper_sum * slope_value).astype(jnp.bfloat16)
    gate_term = jnp.sum(activated * upper_sum, axis=1)
    scaled = (gate_column * slot_y.astype(jnp.float32)).astype(jnp.bfloat16)
    grad_out = jnp.dot(active.T, scaled, preferred_element_type=jnp.float32).astype(jnp.bfloat16)
    grad_in = jnp.dot(slot_x.T, delta_rows, preferred_element_type=jnp.float32).astype(jnp.bfloat16)
    back_rows = jnp.dot(delta_rows, weight_in.T, preferred_element_type=jnp.float32)
    return back_rows, gate_term, grad_in, grad_out


def reference(tokens, out_grad, gate_prob, routing, weight_in, weight_out):
    slot_count = N_SEQ * CAP_SRC
    chosen, slots = slot_table(routing)
    token_index = (jnp.arange(TOKENS * TOP, dtype=jnp.int32) // TOP).astype(jnp.int32)
    slot_x = jnp.zeros((EXPERTS, slot_count, D), jnp.bfloat16).at[chosen, slots].set(tokens[token_index])
    slot_y = jnp.zeros((EXPERTS, slot_count, D), jnp.bfloat16).at[chosen, slots].set(out_grad[token_index])
    slot_gate = jnp.zeros((EXPERTS, slot_count), jnp.bfloat16).at[chosen, slots].set(gate_prob.reshape(-1))
    back_rows, gate_term, grad_in, grad_out = lax.map(expert_backward, (slot_x, slot_y, slot_gate, weight_in, weight_out))
    grad_tokens = jnp.sum(back_rows[chosen, slots].reshape(TOKENS, TOP, D), axis=1).astype(jnp.bfloat16)
    grad_gate = gate_term[chosen, slots].reshape(TOKENS, TOP)
    return grad_tokens, grad_gate, grad_in, grad_out
```

```python
import functools

import jax
import jax.numpy as jnp
from jax import lax
from jax.experimental import pallas as pl
from jax.experimental.pallas import tpu as pltpu
from jax.sharding import PartitionSpec as P

MESH = pl.DeviceIdType.MESH
BF16, F32 = jnp.bfloat16, jnp.float32
gelu_scale = 0.7978845608028654
gelu_cubic = 0.044715


def gelu_parts(pre_act):
    square = pre_act * pre_act
    tangent = jnp.tanh(gelu_scale * pre_act * (1.0 + gelu_cubic * square))
    half = 0.5 * (1.0 + tangent)
    slope = half + 0.5 * pre_act * (1.0 - tangent * tangent) * gelu_scale * (
        1.0 + 3.0 * gelu_cubic * square
    )
    return pre_act * half, slope


def dot(a, b, over):
    return lax.dot_general(a, b, ((over[:1], over[1:]), ((), ())), preferred_element_type=F32)


def split(value):
    high = value.astype(BF16)
    return high, (value - high.astype(F32)).astype(BF16)


def kernel(
    ny, nz, route, gate, tok_h, og_h, win_h, wout_h,
    gtok, ggate, gwi_h, gwo_h,
    tok, og, win, wout, xy, sel, part, r1, r2, s1, ad, bk, pb, ys, yr,
    g, gx, gs, gp, gt, gy, tb, zr, gz, gzr, gwi, gwo,
    in_sem, out_sem, ring_send, ring_recv, sib_send, sib_recv,
    r1_send, r1_recv, r2_send, r2_recv, a1_send, a1_recv, a2_send, a2_recv,
    pb_send, pb_recv, y_send, y_recv,
    gx_send, gx_recv, gp_send, gp_recv, gy_send, gy_recv, z_send, z_recv, gz_send, gz_recv,
):
    s, z, x = lax.axis_index("seq"), lax.axis_index("exp"), lax.axis_index("ffn")
    y, c = s // 2, s % 2
    sib = {"seq": s + 1 - 2 * c}
    xa, xb = {"ffn": x + 1 - 2 * (x % 2)}, {"ffn": 3 - x}
    h1, q1 = ((x + 1) // 2) % 2, x // 2
    h2, q2 = x // 2, x % 2
    units = 2 * ny
    cap = xy.shape[4]
    tokens = tok.shape[0]
    hid = win.shape[2]

    def along_y(step):
        return {"seq": ((y + step + ny) % ny) * 2 + c}

    def along_z(step):
        return {"exp": (z + step) % nz}

    def along_x(step):
        return {"ffn": (x + step) % 4}

    def send(src, dst, ssem, rsem, where):
        pltpu.make_async_remote_copy(
            src_ref=src, dst_ref=dst, send_sem=ssem, recv_sem=rsem,
            device_id=where, device_id_type=MESH,
        ).start()

    def done(ref, sem):
        pltpu.make_async_copy(ref, ref, sem).wait()

    loads = [
        pltpu.make_async_copy(a, b, in_sem.at[i])
        for i, (a, b) in enumerate(((tok_h, tok), (og_h, og), (win_h, win), (wout_h, wout)))
    ]
    for load in loads:
        load.start()

    barrier = pltpu.get_barrier_semaphore()
    peers = [sib]
    peers += [along_y(d) for d in range(1, ny)]
    peers += [along_x(d) for d in range(1, 4)]
    peers += [along_z(d) for d in range(1, nz)]
    for peer in peers:
        pl.semaphore_signal(barrier, inc=1, device_id=peer, device_id_type=MESH)

    ids = [route[k : k + 1, :] for k in range(2)]
    probs = [gate[k : k + 1, :].astype(F32) for k in range(2)]
    named = [[r == 2 * z + e for r in ids] for e in range(2)]
    taken = [jnp.where(named[e][0] | named[e][1], 1.0, 0.0) for e in range(2)]
    weight = [
        jnp.where(named[e][0], probs[0], jnp.where(named[e][1], probs[1], 1.0)) for e in range(2)
    ]
    row_at = lax.broadcasted_iota(jnp.int32, (tokens, tokens), 0)
    col_at = lax.broadcasted_iota(jnp.int32, (tokens, tokens), 1)
    earlier = jnp.where(row_at < col_at, 1.0, 0.0).astype(BF16)
    slot_at = lax.broadcasted_iota(jnp.int32, (cap, tokens), 0).astype(F32)
    g[...] = jnp.zeros_like(g)
    loads[0].wait()
    loads[1].wait()
    for e in range(2):
        before = dot(jnp.broadcast_to(taken[e], (16, tokens)).astype(BF16), earlier, (1, 0))
        hit = (before[0:1, :] == slot_at) & (taken[e] > 0.5)
        sel[e] = jnp.where(hit, 1.0, 0.0).astype(BF16)
        scaled_sel = jnp.where(hit, weight[e], 0.0).astype(BF16)
        xy[0, e, 0, c] = dot(sel[e], tok[...], (1, 0)).astype(BF16)
        xy[1, e, 0, c] = dot(scaled_sel, og[...], (1, 0)).astype(BF16)
        if e == 0:
            pl.semaphore_wait(barrier, len(peers))
        reach = (ny // 2, ny // 2 - 1) if e == 0 else (ny // 2 - 1, ny // 2)
        own = xy.at[:, e, 0, c]
        send(own, own, sib_send, sib_recv.at[e, 0], sib)
        if reach[0] > 0:
            send(own, xy.at[:, e, 1, c], ring_send, ring_recv.at[e, 1], along_y(-1))
        if reach[1] > 0:
            send(own, xy.at[:, e, ny - 1, c], ring_send, ring_recv.at[e, ny - 1], along_y(1))
    loads[2].wait()
    loads[3].wait()

    def far(i):
        odd = i % 2
        return odd * ((i + 1) // 2) + (1 - odd) * ((ny - i // 2) % ny)

    def unit(u):
        e = u // ny
        i = u - e * ny
        return e, far(i + e * (ny - 1 - 2 * i))

    def pass_on(e, j):
        reach = (ny // 2, ny // 2 - 1) if e == 0 else (ny // 2 - 1, ny // 2)
        here = xy.at[:, e, j, c]
        done(here, ring_recv.at[e, j])
        send(here, here, sib_send, sib_recv.at[e, j], sib)

        @pl.when((j <= reach[0]) & (j < reach[0]))
        def _():
            send(here, xy.at[:, e, j + 1, c], ring_send, ring_recv.at[e, j + 1], along_y(-1))

        @pl.when((j >= ny - reach[1]) & (j > ny - reach[1]))
        def _():
            send(here, xy.at[:, e, j - 1, c], ring_send, ring_recv.at[e, j - 1], along_y(1))

    def products(u):
        e, j = unit(u)
        done(xy.at[:, e, j, 0], sib_recv.at[e, j])
        values = (
            dot(xy[0, e, j].reshape(2 * cap, -1), win[e], (1, 0)).astype(BF16),
            dot(xy[1, e, j].reshape(2 * cap, -1), wout[e], (1, 1)).astype(BF16),
        )
        for half in range(2):
            for b in range(4):
                for a in range(2):
                    part[u, half, b, a] = values[a][
                        half * cap : (half + 1) * cap, b * 128 : (b + 1) * 128
                    ]
        send(part.at[u, 0, pl.ds(2 * (1 - h1), 2)], r1.at[u, 0], r1_send, r1_recv.at[u], xa)
        send(part.at[u, 1, pl.ds(2 * (1 - h2), 2)], r1.at[u, 1], r1_send, r1_recv.at[u], xb)

    def halve(u):
        done(r1.at[u], r1_recv.at[u])
        for half, (h, q, to) in enumerate(((h1, q1, xb), (h2, q2, xa))):
            s1[u, half] = (
                part[u, half, 2 * h + 1 - q].astype(F32) + r1[u, half, 1 - q].astype(F32)
            ).astype(BF16)
            send(s1.at[u, half], r2.at[u, half], r2_send, r2_recv.at[u], to)

    def activate(u):
        e, j = unit(u)
        done(r2.at[u], r2_recv.at[u])
        terms = []
        for half, (h, q, to) in enumerate(((h1, q1, xb), (h2, q2, xa))):
            total = (
                part[u, half, 2 * h + q].astype(F32)
                + r1[u, half, q].astype(F32)
                + r2[u, half].astype(F32)
            )
            activated, slope = gelu_parts(total[0])
            ad[e, 2 * h + q, 0, j, half] = activated.astype(BF16)
            ad[e, 2 * h + q, 1, j, half] = (total[1] * slope).astype(BF16)
            piece = ad.at[e, 2 * h + q, :, j, half]
            send(piece, piece, a1_send, a1_recv.at[u], to)
            terms.append(activated * total[1])
        high, low = split(jnp.concatenate(terms, axis=0))
        ones = jnp.ones((16, 2 * 128), BF16)
        summed = dot(ones, jnp.concatenate((high, low), axis=1), (1, 1))
        g[pl.ds(8 * j + e, 1), 0 : 2 * cap] = summed[0:1, :]

    def widen(u):
        e, j = unit(u)
        done(r2.at[u], a1_recv.at[u])
        for half, (h, to) in enumerate(((h1, xa), (h2, xb))):
            piece = ad.at[e, pl.ds(2 * h, 2), :, j, half]
            send(piece, piece, a2_send, a2_recv.at[u], to)

    def back(u):
        e, j = unit(u)
        done(r1.at[u], a2_recv.at[u])
        delta = jnp.concatenate(
            [ad[e, b, 1, j].reshape(2 * cap, 128) for b in range(4)], axis=1
        )
        bk[u] = dot(delta, win[e], (1, 1)).astype(BF16).reshape(2, cap, -1)
        send(bk.at[u, 1 - c], pb.at[u], pb_send, pb_recv.at[u], sib)

    def deliver(u):
        e, j = unit(u)
        done(pb.at[u], pb_recv.at[u])
        both = (bk[u, c].astype(F32) + pb[u].astype(F32)).astype(BF16)

        @pl.when(j == 0)
        def _():
            yr[e, 0] = both

        @pl.when(j > 0)
        def _():
            ys[u] = both
            send(ys.at[u], yr.at[e, j], y_send, y_recv.at[e, j], along_y(j))

    def weight_grads(e, p):
        rows = 2 * ny * cap
        cols = pl.ds(p * (hid // 2), hid // 2)
        act, delta = (
            jnp.concatenate([ad[e, 2 * p + b, a].reshape(rows, 128) for b in range(2)], axis=1)
            for a in range(2)
        )
        gwi[e, :, cols] = dot(xy[0, e].reshape(rows, -1), delta, (0, 0)).astype(BF16)
        gwo[e, cols, :] = dot(act, xy[1, e].reshape(rows, -1), (0, 0)).astype(BF16)

    def store_grads(e):
        return [
            pltpu.make_async_copy(gwi.at[e], gwi_h.at[e], out_sem.at[e, 0]),
            pltpu.make_async_copy(gwo.at[e], gwo_h.at[e], out_sem.at[e, 1]),
        ]

    def step(k, carry):
        def stage(lag, work):
            @pl.when((k >= lag) & (k < units + lag))
            def _():
                work(k - lag)

        stage(1, halve)
        stage(2, activate)
        stage(3, widen)
        stage(0, products)

        @pl.when(k < ny - 1)
        def _():
            pass_on(0, far(k + 1))

        @pl.when((k > 0) & (k < ny))
        def _():
            pass_on(1, far(k))

        stage(4, back)
        stage(5, deliver)

        @pl.when(k == units + 1)
        def _():
            for d in range(1, 4):
                send(g, gx.at[d - 1], gx_send, gx_recv, along_x(d))

        @pl.when(k == units + 2)
        def _():
            done(gx, gx_recv)
            gs[...] = g[...] + gx[0] + gx[1] + gx[2]
            send(gs, gp, gp_send, gp_recv, sib)

        @pl.when(k == units + 3)
        def _():
            done(gp, gp_recv)
            gt[...] = (gs[...] + gp[...]).reshape(gt.shape)
            gy[0] = gt[0]
            for d in range(1, ny):
                send(gt.at[d], gy.at[d], gy_send, gy_recv, along_y(d))

        for p in range(2):
            @pl.when(k == ny + 4 + p)
            def _():
                weight_grads(0, p)

        @pl.when(k == ny + 6)
        def _():
            for copy in store_grads(0):
                copy.start()

        return carry

    lax.fori_loop(0, units + 5, step, 0)

    rows = []
    for e in range(2):
        for j in range(1, ny):
            done(yr.at[e, j], y_recv.at[e, j])
        rows.append(jnp.sum(yr[e].astype(F32), axis=0).astype(BF16))
    for e in range(2):
        own = dot(sel[e], rows[e], (0, 0))
        total = own if e == 0 else total + own
    tb[...] = total.astype(BF16).reshape(tb.shape)
    for d in range(1, nz):
        send(tb.at[(z + d) % nz], zr.at[d], z_send, z_recv, along_z(d))

    done(gy.at[pl.ds(1, ny - 1)], gy_recv)
    term = jnp.sum(gy[...], axis=0)
    term = jnp.where(c == 0, term[:, 0:cap], term[:, cap : 2 * cap])
    term = jnp.concatenate((term, jnp.zeros_like(term)), axis=0)
    high, low = split(term)
    at_token = []
    for e in range(2):
        value = dot(high, sel[e], (1, 0)) + dot(low, sel[e], (1, 0))
        at_token.append(value[e : e + 1, :] / weight[e])
    gz[...] = jnp.zeros_like(gz)
    for k in range(2):
        gz[k : k + 1, :] = jnp.where(named[0][k], at_token[0], 0.0) + jnp.where(
            named[1][k], at_token[1], 0.0
        )
    for d in range(1, nz):
        send(gz, gzr.at[d], gz_send, gz_recv, along_z(d))

    for p in range(2):
        weight_grads(1, p)
    for copy in store_grads(1):
        copy.start()

    out = tb[z].astype(F32)
    gates = gz[...]
    if nz > 1:
        done(zr.at[pl.ds(1, nz - 1)], z_recv)
        done(gzr.at[pl.ds(1, nz - 1)], gz_recv)
        for d in range(1, nz):
            out = out + zr[d].astype(F32)
            gates = gates + gzr[d]
    gtok[...] = out.astype(BF16)
    mine = gtok.shape[0]
    pick = jnp.where(
        lax.broadcasted_iota(jnp.int32, (mine, tokens), 1)
        == lax.broadcasted_iota(jnp.int32, (mine, tokens), 0) + z * mine,
        1.0,
        0.0,
    ).astype(BF16)
    high, low = split(jnp.concatenate((gates, jnp.zeros_like(gates)), axis=0))
    ggate[...] = (dot(pick, high, (1, 1)) + dot(pick, low, (1, 1)))[:, 0:2]

    done(xy.at[:, :, pl.ds(0, ny - 1), 0], ring_send)
    done(xy.at[:, :, :, 0], sib_send)
    done(r1, r1_send)
    done(r2, r2_send)
    done(r2, a1_send)
    done(r1, a2_send)
    done(pb, pb_send)
    done(ys.at[pl.ds(0, 2 * (ny - 1))], y_send)
    done(gx, gx_send)
    done(gp, gp_send)
    done(gy.at[pl.ds(1, ny - 1)], gy_send)
    if nz > 1:
        done(zr.at[pl.ds(1, nz - 1)], z_send)
        done(gzr.at[pl.ds(1, nz - 1)], gz_send)
    for e in range(2):
        for copy in store_grads(e):
            copy.wait()


def body(ny, nz, tokens, out_grad, gate_prob, routing, weight_in, weight_out):
    tok, width = tokens.shape
    hid = weight_in.shape[2]
    cap = 3 * tok // (2 * nz)
    units = 2 * ny
    mine = tok // nz
    vmem, anywhere = (pl.BlockSpec(memory_space=m) for m in (pltpu.VMEM, pl.ANY))
    buf = pltpu.VMEM
    dma = pltpu.SemaphoreType.DMA
    return pl.pallas_call(
        functools.partial(kernel, ny, nz),
        out_shape=(
            jax.ShapeDtypeStruct((mine, width), BF16),
            jax.ShapeDtypeStruct((mine, 2), F32),
            jax.ShapeDtypeStruct(weight_in.shape, BF16),
            jax.ShapeDtypeStruct(weight_out.shape, BF16),
        ),
        in_specs=[vmem, vmem] + [anywhere] * 4,
        out_specs=(vmem, vmem, anywhere, anywhere),
        scratch_shapes=[
            buf((tok, width), BF16),
            buf((tok, width), BF16),
            buf(weight_in.shape, BF16),
            buf(weight_out.shape, BF16),
            buf((2, 2, ny, 2, cap, width), BF16),
            buf((2, cap, tok), BF16),
            buf((units, 2, 4, 2, cap, 128), BF16),
            buf((units, 2, 2, 2, cap, 128), BF16),
            buf((units, 2, 2, cap, 128), BF16),
            buf((units, 2, 2, cap, 128), BF16),
            buf((2, 4, 2, ny, 2, cap, 128), BF16),
            buf((units, 2, cap, width), BF16),
            buf((units, cap, width), BF16),
            buf((units, cap, width), BF16),
            buf((2, ny, cap, width), BF16),
            buf((8 * ny, 128), F32),
            buf((3, 8 * ny, 128), F32),
            buf((8 * ny, 128), F32),
            buf((8 * ny, 128), F32),
            buf((ny, 8, 128), F32),
            buf((ny, 8, 128), F32),
            buf((nz, mine, width), BF16),
            buf((nz, mine, width), BF16),
            buf((8, tok), F32),
            buf((nz, 8, tok), F32),
            buf(weight_in.shape, BF16),
            buf(weight_out.shape, BF16),
            dma((4,)),
            dma((2, 2)),
            dma,
            dma((2, ny)),
            dma,
            dma((2, ny)),
            dma,
            dma((units,)),
            dma,
            dma((units,)),
            dma,
            dma((units,)),
            dma,
            dma((units,)),
            dma,
            dma((units,)),
            dma,
            dma((2, ny)),
            dma,
            dma,
            dma,
            dma,
            dma,
            dma,
            dma,
            dma,
            dma,
            dma,
        ],
        compiler_params=pltpu.CompilerParams(
            collective_id=0, has_side_effects=True, vmem_limit_bytes=48 * 2**20
        ),
        name="expert_backward",
    )(routing.T, gate_prob.T, tokens, out_grad, weight_in, weight_out)


def solution(mesh):
    ny, nz = mesh.shape["seq"] // 2, mesh.shape["exp"]
    return jax.shard_map(
        functools.partial(body, ny, nz),
        mesh=mesh,
        in_specs=(
            P("seq", "ffn"),
            P("seq", "ffn"),
            P("seq", None),
            P("seq", None),
            P("exp", "ffn", "seq"),
            P("exp", "seq", "ffn"),
        ),
        out_specs=(
            P(("seq", "exp"), "ffn"),
            P(("seq", "exp"), None),
            P("exp", "ffn", "seq"),
            P("exp", "seq", "ffn"),
        ),
        check_vma=False,
    )
```

```python
import functools

import jax
import jax.numpy as jnp
from jax import lax
from jax.experimental import pallas as pl
from jax.experimental.pallas import tpu as pltpu
from jax.sharding import PartitionSpec as P

MESH = pl.DeviceIdType.MESH
BF16, F32 = jnp.bfloat16, jnp.float32
gelu_scale = 0.7978845608028654
gelu_cubic = 0.044715
VMEM_BYTES = 62 * 2**20
LAGS = (2, 4, 6, 8, 9)
SECOND = 5


def gelu_parts(pre_act):
    square = pre_act * pre_act
    tangent = jnp.tanh(gelu_scale * pre_act * (1.0 + gelu_cubic * square))
    half = 0.5 * (1.0 + tangent)
    slope = half + 0.5 * pre_act * (1.0 - tangent * tangent) * gelu_scale * (
        1.0 + 3.0 * gelu_cubic * square
    )
    return pre_act * half, slope


def dot(a, b, over):
    return lax.dot_general(a, b, ((over[:1], over[1:]), ((), ())), preferred_element_type=F32)


def split(value):
    high = value.astype(BF16)
    return high, (value - high.astype(F32)).astype(BF16)


def kernel(
    ny, nz, route, gate, tok_h, og_h, win_h, wout_h,
    gtok, ggate, gwi_h, gwo_h,
    tok, og, win, wout, xy, sel, part, r1, r2, s1, ad, bk, pb, ys, yr,
    g, gx, gs, gp, gt, gy, tb, zr, gz, gzr, gwi, gwo,
    in_sem, out_sem, ring_send, ring_recv, sib_send, sib_recv,
    r1_send, r1_recv, r2_send, r2_recv, a1_send, a1_recv, a2_send, a2_recv,
    pb_send, pb_recv, y_send, y_recv,
    gx_send, gx_recv, gp_send, gp_recv, gy_send, gy_recv, z_send, z_recv, gz_send, gz_recv,
):
    s, z, x = lax.axis_index("seq"), lax.axis_index("exp"), lax.axis_index("ffn")
    y, c = s // 2, s % 2
    sib = {"seq": s + 1 - 2 * c}
    xa, xb = {"ffn": x + 1 - 2 * (x % 2)}, {"ffn": 3 - x}
    h1, q1 = ((x + 1) // 2) % 2, x // 2
    h2, q2 = x // 2, x % 2
    units = 2 * ny
    cap = xy.shape[4]
    tokens = tok.shape[0]
    hid = win.shape[2]

    def along_y(step):
        return {"seq": ((y + step + ny) % ny) * 2 + c}

    def along_z(step):
        return {"exp": (z + step) % nz}

    def along_x(step):
        return {"ffn": (x + step) % 4}

    def send(src, dst, ssem, rsem, where):
        pltpu.make_async_remote_copy(
            src_ref=src, dst_ref=dst, send_sem=ssem, recv_sem=rsem,
            device_id=where, device_id_type=MESH,
        ).start()

    def done(ref, sem):
        pltpu.make_async_copy(ref, ref, sem).wait()

    loads = [
        pltpu.make_async_copy(a, b, in_sem.at[i])
        for i, (a, b) in enumerate(((tok_h, tok), (og_h, og), (win_h, win), (wout_h, wout)))
    ]
    for load in loads:
        load.start()

    barrier = pltpu.get_barrier_semaphore()
    peers = [sib]
    peers += [along_y(d) for d in range(1, ny)]
    peers += [along_x(d) for d in range(1, 4)]
    peers += [along_z(d) for d in range(1, nz)]
    for peer in peers:
        pl.semaphore_signal(barrier, inc=1, device_id=peer, device_id_type=MESH)

    def spread(e):
        reach = (ny // 2, ny // 2 - 1) if e == 0 else (ny // 2 - 1, ny // 2)
        own = xy.at[:, e, 0, c]
        send(own, own, sib_send, sib_recv.at[e, 0], sib)
        if reach[0] > 0:
            send(own, xy.at[:, e, 1, c], ring_send, ring_recv.at[e, 1], along_y(-1))
        if reach[1] > 0:
            send(own, xy.at[:, e, ny - 1, c], ring_send, ring_recv.at[e, ny - 1], along_y(1))

    ids = [route[k : k + 1, :] for k in range(2)]
    probs = [gate[k : k + 1, :].astype(F32) for k in range(2)]
    named = [[r == 2 * z + e for r in ids] for e in range(2)]
    taken = [jnp.where(named[e][0] | named[e][1], 1.0, 0.0) for e in range(2)]
    weight = [
        jnp.where(named[e][0], probs[0], jnp.where(named[e][1], probs[1], 1.0)) for e in range(2)
    ]
    row_at = lax.broadcasted_iota(jnp.int32, (tokens, tokens), 0)
    col_at = lax.broadcasted_iota(jnp.int32, (tokens, tokens), 1)
    earlier = jnp.where(row_at < col_at, 1.0, 0.0).astype(BF16)
    slot_at = lax.broadcasted_iota(jnp.int32, (cap, tokens), 0).astype(F32)
    g[...] = jnp.zeros_like(g)
    loads[0].wait()
    loads[1].wait()
    for e in range(2):
        before = dot(jnp.broadcast_to(taken[e], (16, tokens)).astype(BF16), earlier, (1, 0))
        hit = (before[0:1, :] == slot_at) & (taken[e] > 0.5)
        sel[e] = jnp.where(hit, 1.0, 0.0).astype(BF16)
        scaled_sel = jnp.where(hit, weight[e], 0.0).astype(BF16)
        xy[0, e, 0, c] = dot(sel[e], tok[...], (1, 0)).astype(BF16)
        xy[1, e, 0, c] = dot(scaled_sel, og[...], (1, 0)).astype(BF16)
        if e == 0:
            pl.semaphore_wait(barrier, len(peers))
        if e == 0:
            spread(0)
    loads[2].wait()
    loads[3].wait()

    def far(i):
        odd = i % 2
        return odd * ((i + 1) // 2) + (1 - odd) * ((ny - i // 2) % ny)

    def unit(u):
        e = u // ny
        i = u - e * ny
        return e, far((i + e) % ny)

    def pass_on(e, j):
        reach = (ny // 2, ny // 2 - 1) if e == 0 else (ny // 2 - 1, ny // 2)
        here = xy.at[:, e, j, c]
        done(here, ring_recv.at[e, j])
        send(here, here, sib_send, sib_recv.at[e, j], sib)

        @pl.when((j <= reach[0]) & (j < reach[0]))
        def _():
            send(here, xy.at[:, e, j + 1, c], ring_send, ring_recv.at[e, j + 1], along_y(-1))

        @pl.when((j >= ny - reach[1]) & (j > ny - reach[1]))
        def _():
            send(here, xy.at[:, e, j - 1, c], ring_send, ring_recv.at[e, j - 1], along_y(1))

    def products(u):
        e, j = unit(u)
        done(xy.at[:, e, j, 0], sib_recv.at[e, j])
        values = (
            dot(xy[0, e, j].reshape(2 * cap, -1), win[e], (1, 0)).astype(BF16),
            dot(xy[1, e, j].reshape(2 * cap, -1), wout[e], (1, 1)).astype(BF16),
        )
        for half in range(2):
            for b in range(4):
                for a in range(2):
                    part[u, half, b, a] = values[a][
                        half * cap : (half + 1) * cap, b * 128 : (b + 1) * 128
                    ]
        send(part.at[u, 0, pl.ds(2 * (1 - h1), 2)], r1.at[u, 0], r1_send, r1_recv.at[u], xa)
        send(part.at[u, 1, pl.ds(2 * (1 - h2), 2)], r1.at[u, 1], r1_send, r1_recv.at[u], xb)

    def halve(u):
        done(r1.at[u], r1_recv.at[u])
        for half, (h, q, to) in enumerate(((h1, q1, xb), (h2, q2, xa))):
            s1[u, half] = (
                part[u, half, 2 * h + 1 - q].astype(F32) + r1[u, half, 1 - q].astype(F32)
            ).astype(BF16)
            send(s1.at[u, half], r2.at[u, half], r2_send, r2_recv.at[u], to)

    def activate(u):
        e, j = unit(u)
        done(r2.at[u], r2_recv.at[u])
        terms = []
        for half, (h, q, to) in enumerate(((h1, q1, xb), (h2, q2, xa))):
            total = (
                part[u, half, 2 * h + q].astype(F32)
                + r1[u, half, q].astype(F32)
                + r2[u, half].astype(F32)
            )
            activated, slope = gelu_parts(total[0])
            ad[e, 2 * h + q, 0, j, half] = activated.astype(BF16)
            ad[e, 2 * h + q, 1, j, half] = (total[1] * slope).astype(BF16)
            piece = ad.at[e, 2 * h + q, :, j, half]
            send(piece, piece, a1_send, a1_recv.at[u], to)
            terms.append(activated * total[1])
        high, low = split(jnp.concatenate(terms, axis=0))
        ones = jnp.ones((16, 2 * 128), BF16)
        summed = dot(ones, jnp.concatenate((high, low), axis=1), (1, 1))
        g[pl.ds(8 * j + e, 1), 0 : 2 * cap] = summed[0:1, :]

    def widen(u):
        e, j = unit(u)
        done(r2.at[u], a1_recv.at[u])
        for half, (h, to) in enumerate(((h1, xa), (h2, xb))):
            piece = ad.at[e, pl.ds(2 * h, 2), :, j, half]
            send(piece, piece, a2_send, a2_recv.at[u], to)

    def back(u):
        e, j = unit(u)
        done(r1.at[u], a2_recv.at[u])
        delta = jnp.concatenate(
            [ad[e, b, 1, j].reshape(2 * cap, 128) for b in range(4)], axis=1
        )
        bk[u] = dot(delta, win[e], (1, 1)).astype(BF16).reshape(2, cap, -1)
        send(bk.at[u, 1 - c], pb.at[u], pb_send, pb_recv.at[u], sib)

    def deliver(u):
        e, j = unit(u)
        done(pb.at[u], pb_recv.at[u])
        both = (bk[u, c].astype(F32) + pb[u].astype(F32)).astype(BF16)

        @pl.when(j == 0)
        def _():
            yr[e, 0] = both

        @pl.when(j > 0)
        def _():
            ys[u] = both
            send(ys.at[u], yr.at[e, j], y_send, y_recv.at[e, j], along_y(j))

    def weight_grads(e, p):
        rows = 2 * ny * cap
        cols = pl.ds(p * (hid // 2), hid // 2)
        act, delta = (
            jnp.concatenate([ad[e, 2 * p + b, a].reshape(rows, 128) for b in range(2)], axis=1)
            for a in range(2)
        )
        gwi[e, :, cols] = dot(xy[0, e].reshape(rows, -1), delta, (0, 0)).astype(BF16)
        gwo[e, cols, :] = dot(act, xy[1, e].reshape(rows, -1), (0, 0)).astype(BF16)

    def store_grads(e):
        return [
            pltpu.make_async_copy(gwi.at[e], gwi_h.at[e], out_sem.at[e, 0]),
            pltpu.make_async_copy(gwo.at[e], gwo_h.at[e], out_sem.at[e, 1]),
        ]

    def step(k, carry):
        def stage(lag, work):
            @pl.when((k >= lag) & (k < units + lag))
            def _():
                work(k - lag)

        stage(LAGS[0], halve)
        stage(LAGS[1], activate)
        stage(LAGS[2], widen)
        stage(0, products)

        @pl.when(k < ny - 1)
        def _():
            pass_on(0, far(k + 1))

        @pl.when(k == SECOND)
        def _():
            spread(1)

        @pl.when((k > SECOND) & (k < SECOND + ny))
        def _():
            pass_on(1, far(k - SECOND))

        stage(LAGS[3], back)
        stage(LAGS[4], deliver)

        @pl.when(k == units - 1 + LAGS[1])
        def _():
            for d in range(1, 4):
                send(g, gx.at[d - 1], gx_send, gx_recv, along_x(d))

        @pl.when(k == units - 1 + LAGS[2])
        def _():
            done(gx, gx_recv)
            gs[...] = g[...] + gx[0] + gx[1] + gx[2]
            send(gs, gp, gp_send, gp_recv, sib)

        @pl.when(k == units - 1 + LAGS[3])
        def _():
            done(gp, gp_recv)
            gt[...] = (gs[...] + gp[...]).reshape(gt.shape)
            gy[0] = gt[0]
            for d in range(1, ny):
                send(gt.at[d], gy.at[d], gy_send, gy_recv, along_y(d))

        for p in range(2):
            @pl.when(k == ny + LAGS[3] + p)
            def _():
                weight_grads(0, p)

        @pl.when(k == ny + LAGS[3] + 2)
        def _():
            for copy in store_grads(0):
                copy.start()

        return carry

    lax.fori_loop(0, units + LAGS[4], step, 0)

    rows = []
    for e in range(2):
        for j in range(1, ny):
            done(yr.at[e, j], y_recv.at[e, j])
        rows.append(jnp.sum(yr[e].astype(F32), axis=0).astype(BF16))
    for e in range(2):
        own = dot(sel[e], rows[e], (0, 0))
        total = own if e == 0 else total + own
    tb[...] = total.astype(BF16).reshape(tb.shape)
    for d in range(1, nz):
        send(tb.at[(z + d) % nz], zr.at[d], z_send, z_recv, along_z(d))

    done(gy.at[pl.ds(1, ny - 1)], gy_recv)
    term = jnp.sum(gy[...], axis=0)
    term = jnp.where(c == 0, term[:, 0:cap], term[:, cap : 2 * cap])
    term = jnp.concatenate((term, jnp.zeros_like(term)), axis=0)
    high, low = split(term)
    at_token = []
    for e in range(2):
        value = dot(high, sel[e], (1, 0)) + dot(low, sel[e], (1, 0))
        at_token.append(value[e : e + 1, :] / weight[e])
    gz[...] = jnp.zeros_like(gz)
    for k in range(2):
        gz[k : k + 1, :] = jnp.where(named[0][k], at_token[0], 0.0) + jnp.where(
            named[1][k], at_token[1], 0.0
        )
    for d in range(1, nz):
        send(gz, gzr.at[d], gz_send, gz_recv, along_z(d))

    for p in range(2):
        weight_grads(1, p)
    for copy in store_grads(1):
        copy.start()

    out = tb[z].astype(F32)
    gates = gz[...]
    if nz > 1:
        done(zr.at[pl.ds(1, nz - 1)], z_recv)
        done(gzr.at[pl.ds(1, nz - 1)], gz_recv)
        for d in range(1, nz):
            out = out + zr[d].astype(F32)
            gates = gates + gzr[d]
    gtok[...] = out.astype(BF16)
    mine = gtok.shape[0]
    pick = jnp.where(
        lax.broadcasted_iota(jnp.int32, (mine, tokens), 1)
        == lax.broadcasted_iota(jnp.int32, (mine, tokens), 0) + z * mine,
        1.0,
        0.0,
    ).astype(BF16)
    high, low = split(jnp.concatenate((gates, jnp.zeros_like(gates)), axis=0))
    ggate[...] = (dot(high, pick, (1, 1)) + dot(low, pick, (1, 1)))[0:2, :]

    done(xy.at[:, :, pl.ds(0, ny - 1), 0], ring_send)
    done(xy.at[:, :, :, 0], sib_send)
    done(r1, r1_send)
    done(r2, r2_send)
    done(r2, a1_send)
    done(r1, a2_send)
    done(pb, pb_send)
    done(ys.at[pl.ds(0, 2 * (ny - 1))], y_send)
    done(gx, gx_send)
    done(gp, gp_send)
    done(gy.at[pl.ds(1, ny - 1)], gy_send)
    if nz > 1:
        done(zr.at[pl.ds(1, nz - 1)], z_send)
        done(gzr.at[pl.ds(1, nz - 1)], gz_send)
    for e in range(2):
        for copy in store_grads(e):
            copy.wait()


def hand_over(*refs):
    given, out, held, sems = refs[:4], refs[4:8], refs[8:12], refs[12]
    loads = [pltpu.make_async_copy(given[i], held[i], sems.at[0, i]) for i in range(4)]
    stores = [pltpu.make_async_copy(held[i], out[i], sems.at[1, i]) for i in range(4)]
    for load in loads:
        load.start()
    for load, store in zip(loads, stores):
        load.wait()
        store.start()
    for store in stores:
        store.wait()


def body(ny, nz, tokens, out_grad, gate_prob, routing, weight_in, weight_out):
    tok, width = tokens.shape
    hid = weight_in.shape[2]
    cap = 3 * tok // (2 * nz)
    units = 2 * ny
    mine = tok // nz
    vmem, anywhere = (pl.BlockSpec(memory_space=m) for m in (pltpu.VMEM, pl.ANY))
    buf = pltpu.VMEM
    dma = pltpu.SemaphoreType.DMA
    results = pl.pallas_call(
        functools.partial(kernel, ny, nz),
        out_shape=(
            jax.ShapeDtypeStruct((mine, width), BF16),
            jax.ShapeDtypeStruct((2, mine), F32),
            jax.ShapeDtypeStruct(weight_in.shape, BF16),
            jax.ShapeDtypeStruct(weight_out.shape, BF16),
        ),
        in_specs=[vmem, vmem] + [anywhere] * 4,
        out_specs=(vmem, vmem, anywhere, anywhere),
        scratch_shapes=[
            buf((tok, width), BF16),
            buf((tok, width), BF16),
            buf(weight_in.shape, BF16),
            buf(weight_out.shape, BF16),
            buf((2, 2, ny, 2, cap, width), BF16),
            buf((2, cap, tok), BF16),
            buf((units, 2, 4, 2, cap, 128), BF16),
            buf((units, 2, 2, 2, cap, 128), BF16),
            buf((units, 2, 2, cap, 128), BF16),
            buf((units, 2, 2, cap, 128), BF16),
            buf((2, 4, 2, ny, 2, cap, 128), BF16),
            buf((units, 2, cap, width), BF16),
            buf((units, cap, width), BF16),
            buf((units, cap, width), BF16),
            buf((2, ny, cap, width), BF16),
            buf((8 * ny, 128), F32),
            buf((3, 8 * ny, 128), F32),
            buf((8 * ny, 128), F32),
            buf((8 * ny, 128), F32),
            buf((ny, 8, 128), F32),
            buf((ny, 8, 128), F32),
            buf((nz, mine, width), BF16),
            buf((nz, mine, width), BF16),
            buf((8, tok), F32),
            buf((nz, 8, tok), F32),
            buf(weight_in.shape, BF16),
            buf(weight_out.shape, BF16),
            dma((4,)),
            dma((2, 2)),
            dma,
            dma((2, ny)),
            dma,
            dma((2, ny)),
            dma,
            dma((units,)),
            dma,
            dma((units,)),
            dma,
            dma((units,)),
            dma,
            dma((units,)),
            dma,
            dma((units,)),
            dma,
            dma((2, ny)),
            dma,
            dma,
            dma,
            dma,
            dma,
            dma,
            dma,
            dma,
            dma,
            dma,
        ],
        compiler_params=pltpu.CompilerParams(
            collective_id=0, has_side_effects=True, vmem_limit_bytes=VMEM_BYTES
        ),
        name="expert_backward",
    )(routing.T, gate_prob.T, tokens, out_grad, weight_in, weight_out)
    gtok, ggate, gwi, gwo = pl.pallas_call(
        hand_over,
        out_shape=tuple(jax.ShapeDtypeStruct(r.shape, r.dtype) for r in results),
        in_specs=[anywhere] * 4,
        out_specs=(anywhere,) * 4,
        scratch_shapes=[buf(r.shape, r.dtype) for r in results] + [dma((2, 4))],
        compiler_params=pltpu.CompilerParams(vmem_limit_bytes=VMEM_BYTES),
        name="hand_over",
    )(*results)
    return gtok, ggate.T, gwi, gwo


def solution(mesh):
    ny, nz = mesh.shape["seq"] // 2, mesh.shape["exp"]
    return jax.shard_map(
        functools.partial(body, ny, nz),
        mesh=mesh,
        in_specs=(
            P("seq", "ffn"),
            P("seq", "ffn"),
            P("seq", None),
            P("seq", None),
            P("exp", "ffn", "seq"),
            P("exp", "seq", "ffn"),
        ),
        out_specs=(
            P(("seq", "exp"), "ffn"),
            P(("seq", "exp"), None),
            P("exp", "ffn", "seq"),
            P("exp", "seq", "ffn"),
        ),
        check_vma=False,
    )
```

```python
import functools

import jax
import jax.numpy as jnp
from jax import lax
from jax.experimental import pallas as pl
from jax.experimental.pallas import tpu as pltpu
from jax.sharding import PartitionSpec as P

MESH = pl.DeviceIdType.MESH
BF16, F32 = jnp.bfloat16, jnp.float32
gelu_scale = 0.7978845608028654
gelu_cubic = 0.044715
VMEM_BYTES = 62 * 2**20
LAGS = (2, 4, 6, 8, 9)
SECOND = 1


def gelu_parts(pre_act):
    square = pre_act * pre_act
    tangent = jnp.tanh(gelu_scale * pre_act * (1.0 + gelu_cubic * square))
    half = 0.5 * (1.0 + tangent)
    slope = half + 0.5 * pre_act * (1.0 - tangent * tangent) * gelu_scale * (
        1.0 + 3.0 * gelu_cubic * square
    )
    return pre_act * half, slope


def dot(a, b, over):
    return lax.dot_general(a, b, ((over[:1], over[1:]), ((), ())), preferred_element_type=F32)


def split(value):
    high = value.astype(BF16)
    return high, (value - high.astype(F32)).astype(BF16)


def kernel(
    ny, nz, route, gate, tok_h, og_h, win_h, wout_h,
    gtok, ggate, gwi_h, gwo_h,
    tok, og, win, wout, xy, sel, part, r1, r2, s1, act, dlt, bk, pb, ys, yr,
    g, gx, gs, gp, gt, gy, tb, zr, gz, gzr, gwi, gwo,
    in_sem, out_sem, ring_send, ring_recv, sib_send, sib_recv,
    r1_send, r1_recv, r2_send, r2_recv, d1_send, d1_recv, d2_send, d2_recv,
    a1_send, a1_recv, a2_send, a2_recv,
    pb_send, pb_recv, y_send, y_recv,
    gx_send, gx_recv, gp_send, gp_recv, gy_send, gy_recv, z_send, z_recv, gz_send, gz_recv,
):
    s, z, x = lax.axis_index("seq"), lax.axis_index("exp"), lax.axis_index("ffn")
    y, c = s // 2, s % 2
    sib = {"seq": s + 1 - 2 * c}
    xa, xb = {"ffn": x + 1 - 2 * (x % 2)}, {"ffn": 3 - x}
    h1, q1 = ((x + 1) // 2) % 2, x // 2
    h2, q2 = x // 2, x % 2
    units = 2 * ny
    cap = xy.shape[4]
    tokens = tok.shape[0]
    hid = win.shape[2]

    def along_y(step):
        return {"seq": ((y + step + ny) % ny) * 2 + c}

    def along_z(step):
        return {"exp": (z + step) % nz}

    def along_x(step):
        return {"ffn": (x + step) % 4}

    def send(src, dst, ssem, rsem, where):
        pltpu.make_async_remote_copy(
            src_ref=src, dst_ref=dst, send_sem=ssem, recv_sem=rsem,
            device_id=where, device_id_type=MESH,
        ).start()

    def done(ref, sem):
        pltpu.make_async_copy(ref, ref, sem).wait()

    loads = [
        pltpu.make_async_copy(a, b, in_sem.at[i])
        for i, (a, b) in enumerate(((tok_h, tok), (og_h, og), (win_h, win), (wout_h, wout)))
    ]
    for load in loads:
        load.start()

    barrier = pltpu.get_barrier_semaphore()
    peers = [sib]
    peers += [along_y(d) for d in range(1, ny)]
    peers += [along_x(d) for d in range(1, 4)]
    peers += [along_z(d) for d in range(1, nz)]
    for peer in peers:
        pl.semaphore_signal(barrier, inc=1, device_id=peer, device_id_type=MESH)

    def spread(e):
        reach = (ny // 2, ny // 2 - 1) if e == 0 else (ny // 2 - 1, ny // 2)
        own = xy.at[:, e, 0, c]
        if reach[0] > 0:
            send(own, xy.at[:, e, 1, c], ring_send, ring_recv.at[e, 1], along_y(-1))
        if reach[1] > 0:
            send(own, xy.at[:, e, ny - 1, c], ring_send, ring_recv.at[e, ny - 1], along_y(1))

    ids = [route[k : k + 1, :] for k in range(2)]
    probs = [gate[k : k + 1, :].astype(F32) for k in range(2)]
    named = [[r == 2 * z + e for r in ids] for e in range(2)]
    taken = [jnp.where(named[e][0] | named[e][1], 1.0, 0.0) for e in range(2)]
    weight = [
        jnp.where(named[e][0], probs[0], jnp.where(named[e][1], probs[1], 1.0)) for e in range(2)
    ]
    row_at = lax.broadcasted_iota(jnp.int32, (tokens, tokens), 0)
    col_at = lax.broadcasted_iota(jnp.int32, (tokens, tokens), 1)
    earlier = jnp.where(row_at < col_at, 1.0, 0.0).astype(BF16)
    slot_at = lax.broadcasted_iota(jnp.int32, (cap, tokens), 0).astype(F32)
    g[...] = jnp.zeros_like(g)
    loads[0].wait()
    loads[1].wait()
    for e in range(2):
        before = dot(jnp.broadcast_to(taken[e], (16, tokens)).astype(BF16), earlier, (1, 0))
        hit = (before[0:1, :] == slot_at) & (taken[e] > 0.5)
        sel[e] = jnp.where(hit, 1.0, 0.0).astype(BF16)
        scaled_sel = jnp.where(hit, weight[e], 0.0).astype(BF16)
        xy[0, e, 0, c] = dot(sel[e], tok[...], (1, 0)).astype(BF16)
        xy[1, e, 0, c] = dot(scaled_sel, og[...], (1, 0)).astype(BF16)
        if e == 0:
            pl.semaphore_wait(barrier, len(peers))
        own = xy.at[:, e, 0, c]
        send(own, own, sib_send, sib_recv.at[e, 0], sib)
        if e == 0:
            spread(0)
    loads[2].wait()
    loads[3].wait()

    def far(i):
        odd = i % 2
        return odd * ((i + 1) // 2) + (1 - odd) * ((ny - i // 2) % ny)

    def unit(u):
        own = 1 - jnp.minimum(u // 2, 1)
        late = jnp.minimum((u + own * ny) // (ny + 1), 1)
        e = own * u + (1 - own) * late
        i = (1 - own) * ((1 - late) * (u - 1) + late * (units - u))
        return e, far(i)

    def pass_on(e, j):
        reach = (ny // 2, ny // 2 - 1) if e == 0 else (ny // 2 - 1, ny // 2)
        here = xy.at[:, e, j, c]
        done(here, ring_recv.at[e, j])
        send(here, here, sib_send, sib_recv.at[e, j], sib)

        @pl.when((j <= reach[0]) & (j < reach[0]))
        def _():
            send(here, xy.at[:, e, j + 1, c], ring_send, ring_recv.at[e, j + 1], along_y(-1))

        @pl.when((j >= ny - reach[1]) & (j > ny - reach[1]))
        def _():
            send(here, xy.at[:, e, j - 1, c], ring_send, ring_recv.at[e, j - 1], along_y(1))

    def products(u):
        e, j = unit(u)
        done(xy.at[:, e, j, 0], sib_recv.at[e, j])
        values = (
            dot(xy[0, e, j].reshape(2 * cap, -1), win[e], (1, 0)).astype(BF16),
            dot(xy[1, e, j].reshape(2 * cap, -1), wout[e], (1, 1)).astype(BF16),
        )
        for half in range(2):
            for b in range(4):
                for a in range(2):
                    part[u, half, b, a] = values[a][
                        half * cap : (half + 1) * cap, b * 128 : (b + 1) * 128
                    ]
        send(part.at[u, 0, pl.ds(2 * (1 - h1), 2)], r1.at[u, 0], r1_send, r1_recv.at[u], xa)
        send(part.at[u, 1, pl.ds(2 * (1 - h2), 2)], r1.at[u, 1], r1_send, r1_recv.at[u], xb)

    def halve(u):
        done(r1.at[u], r1_recv.at[u])
        for half, (h, q, to) in enumerate(((h1, q1, xb), (h2, q2, xa))):
            s1[u, half] = (
                part[u, half, 2 * h + 1 - q].astype(F32) + r1[u, half, 1 - q].astype(F32)
            ).astype(BF16)
            send(s1.at[u, half], r2.at[u, half], r2_send, r2_recv.at[u], to)

    def activate(u):
        e, j = unit(u)
        done(r2.at[u], r2_recv.at[u])
        terms = []
        for half, (h, q, to) in enumerate(((h1, q1, xb), (h2, q2, xa))):
            total = (
                part[u, half, 2 * h + q].astype(F32)
                + r1[u, half, q].astype(F32)
                + r2[u, half].astype(F32)
            )
            activated, slope = gelu_parts(total[0])
            act[e, 2 * h + q, j, half] = activated.astype(BF16)
            dlt[e, 2 * h + q, j, half] = (total[1] * slope).astype(BF16)
            piece = dlt.at[e, 2 * h + q, j, half]
            send(piece, piece, d1_send, d1_recv.at[u], to)
            terms.append(activated * total[1])
        high, low = split(jnp.concatenate(terms, axis=0))
        ones = jnp.ones((16, 2 * 128), BF16)
        summed = dot(ones, jnp.concatenate((high, low), axis=1), (1, 1))
        g[pl.ds(8 * j + e, 1), 0 : 2 * cap] = summed[0:1, :]

    def widen(u):
        e, j = unit(u)
        done(r2.at[u, 0], d1_recv.at[u])
        for half, (h, to) in enumerate(((h1, xa), (h2, xb))):
            piece = dlt.at[e, pl.ds(2 * h, 2), j, half]
            send(piece, piece, d2_send, d2_recv.at[u], to)

    def share_active(e):
        for half, (h, q, to) in enumerate(((h1, q1, xb), (h2, q2, xa))):
            piece = act.at[e, 2 * h + q, :, half]
            send(piece, piece, a1_send, a1_recv.at[e], to)

    def widen_active(e):
        done(act.at[e, 0], a1_recv.at[e])
        for half, (h, to) in enumerate(((h1, xa), (h2, xb))):
            piece = act.at[e, pl.ds(2 * h, 2), :, half]
            send(piece, piece, a2_send, a2_recv.at[e], to)

    def back(u):
        e, j = unit(u)
        done(r2.at[u], d2_recv.at[u])
        delta = jnp.concatenate(
            [dlt[e, b, j].reshape(2 * cap, 128) for b in range(4)], axis=1
        )
        bk[u] = dot(delta, win[e], (1, 1)).astype(BF16).reshape(2, cap, -1)
        send(bk.at[u, 1 - c], pb.at[u], pb_send, pb_recv.at[u], sib)

    def deliver(u):
        e, j = unit(u)
        done(pb.at[u], pb_recv.at[u])
        both = (bk[u, c].astype(F32) + pb[u].astype(F32)).astype(BF16)

        @pl.when(j == 0)
        def _():
            yr[e, 0] = both

        @pl.when(j > 0)
        def _():
            ys[u] = both
            send(ys.at[u], yr.at[e, j], y_send, y_recv.at[e, j], along_y(j))

    def two_blocks(ref, e, p):
        return jnp.concatenate(
            [ref[e, 2 * p + b].reshape(2 * ny * cap, 128) for b in range(2)], axis=1
        )

    def grad_in(e, p):
        values = xy[0, e].reshape(2 * ny * cap, -1)
        cols = pl.ds(p * (hid // 2), hid // 2)
        gwi[e, :, cols] = dot(values, two_blocks(dlt, e, p), (0, 0)).astype(BF16)

    def grad_out(e, p):
        values = xy[1, e].reshape(2 * ny * cap, -1)
        rows = pl.ds(p * (hid // 2), hid // 2)
        gwo[e, rows, :] = dot(two_blocks(act, e, p), values, (0, 0)).astype(BF16)

    def store_in(e):
        return pltpu.make_async_copy(gwi.at[e], gwi_h.at[e], out_sem.at[e, 0])

    def store_out(e):
        return pltpu.make_async_copy(gwo.at[e], gwo_h.at[e], out_sem.at[e, 1])

    def step(k, carry):
        def stage(lag, work):
            @pl.when((k >= lag) & (k < units + lag))
            def _():
                work(k - lag)

        stage(LAGS[0], halve)
        stage(LAGS[1], activate)
        stage(LAGS[2], widen)
        stage(0, products)

        @pl.when((k > 0) & (k < ny))
        def _():
            pass_on(0, far(k))

        @pl.when(k == SECOND)
        def _():
            spread(1)

        @pl.when((k > SECOND) & (k < SECOND + ny))
        def _():
            pass_on(1, far(k - SECOND))

        stage(LAGS[3], back)
        stage(LAGS[4], deliver)

        @pl.when(k == units - 1 + LAGS[1])
        def _():
            for d in range(1, 4):
                send(g, gx.at[d - 1], gx_send, gx_recv, along_x(d))

        @pl.when(k == units - 1 + LAGS[2])
        def _():
            done(gx, gx_recv)
            gs[...] = g[...] + gx[0] + gx[1] + gx[2]
            send(gs, gp, gp_send, gp_recv, sib)

        @pl.when(k == units - 1 + LAGS[3])
        def _():
            done(gp, gp_recv)
            gt[...] = (gs[...] + gp[...]).reshape(gt.shape)
            gy[0] = gt[0]
            for d in range(1, ny):
                send(gt.at[d], gy.at[d], gy_send, gy_recv, along_y(d))

        @pl.when(k == units)
        def _():
            share_active(0)

        @pl.when(k == units - 1 + LAGS[1])
        def _():
            share_active(1)

        @pl.when(k == units - 1 + LAGS[2])
        def _():
            widen_active(0)

        for p in range(2):
            @pl.when(k == ny + 1 + LAGS[3] + p)
            def _():
                grad_in(0, p)

        @pl.when(k == ny + 3 + LAGS[3])
        def _():
            store_in(0).start()

        return carry

    lax.fori_loop(0, units + LAGS[4], step, 0)
    widen_active(1)

    rows = []
    for e in range(2):
        for j in range(1, ny):
            done(yr.at[e, j], y_recv.at[e, j])
        rows.append(jnp.sum(yr[e].astype(F32), axis=0).astype(BF16))
    for e in range(2):
        own = dot(sel[e], rows[e], (0, 0))
        total = own if e == 0 else total + own
    tb[...] = total.astype(BF16).reshape(tb.shape)
    for d in range(1, nz):
        send(tb.at[(z + d) % nz], zr.at[d], z_send, z_recv, along_z(d))

    done(gy.at[pl.ds(1, ny - 1)], gy_recv)
    term = jnp.sum(gy[...], axis=0)
    term = jnp.where(c == 0, term[:, 0:cap], term[:, cap : 2 * cap])
    term = jnp.concatenate((term, jnp.zeros_like(term)), axis=0)
    high, low = split(term)
    at_token = []
    for e in range(2):
        value = dot(high, sel[e], (1, 0)) + dot(low, sel[e], (1, 0))
        at_token.append(value[e : e + 1, :] / weight[e])
    gz[...] = jnp.zeros_like(gz)
    for k in range(2):
        gz[k : k + 1, :] = jnp.where(named[0][k], at_token[0], 0.0) + jnp.where(
            named[1][k], at_token[1], 0.0
        )
    for d in range(1, nz):
        send(gz, gzr.at[d], gz_send, gz_recv, along_z(d))

    for p in range(2):
        grad_in(1, p)
    store_in(1).start()
    for e in range(2):
        done(act.at[e, pl.ds(0, 2)], a2_recv.at[e])
        for p in range(2):
            grad_out(e, p)
        store_out(e).start()

    out = tb[z].astype(F32)
    gates = gz[...]
    if nz > 1:
        done(zr.at[pl.ds(1, nz - 1)], z_recv)
        done(gzr.at[pl.ds(1, nz - 1)], gz_recv)
        for d in range(1, nz):
            out = out + zr[d].astype(F32)
            gates = gates + gzr[d]
    gtok[...] = out.astype(BF16)
    mine = gtok.shape[0]
    pick = jnp.where(
        lax.broadcasted_iota(jnp.int32, (mine, tokens), 1)
        == lax.broadcasted_iota(jnp.int32, (mine, tokens), 0) + z * mine,
        1.0,
        0.0,
    ).astype(BF16)
    high, low = split(jnp.concatenate((gates, jnp.zeros_like(gates)), axis=0))
    ggate[...] = (dot(high, pick, (1, 1)) + dot(low, pick, (1, 1)))[0:2, :]

    done(xy.at[:, :, pl.ds(0, ny - 1), 0], ring_send)
    done(xy.at[:, :, :, 0], sib_send)
    done(r1, r1_send)
    done(r2, r2_send)
    done(r2.at[:, 0], d1_send)
    done(r2, d2_send)
    done(act.at[:, 0], a1_send)
    done(act.at[:, pl.ds(0, 2)], a2_send)
    done(pb, pb_send)
    done(ys.at[pl.ds(0, 2 * (ny - 1))], y_send)
    done(gx, gx_send)
    done(gp, gp_send)
    done(gy.at[pl.ds(1, ny - 1)], gy_send)
    if nz > 1:
        done(zr.at[pl.ds(1, nz - 1)], z_send)
        done(gzr.at[pl.ds(1, nz - 1)], gz_send)
    for e in range(2):
        store_in(e).wait()
        store_out(e).wait()


def hand_over(*refs):
    given, out, held, sems = refs[:4], refs[4:8], refs[8:12], refs[12]
    loads = [pltpu.make_async_copy(given[i], held[i], sems.at[0, i]) for i in range(4)]
    stores = [pltpu.make_async_copy(held[i], out[i], sems.at[1, i]) for i in range(4)]
    for load in loads:
        load.start()
    for load, store in zip(loads, stores):
        load.wait()
        store.start()
    for store in stores:
        store.wait()


def body(ny, nz, tokens, out_grad, gate_prob, routing, weight_in, weight_out):
    tok, width = tokens.shape
    hid = weight_in.shape[2]
    cap = 3 * tok // (2 * nz)
    units = 2 * ny
    mine = tok // nz
    vmem, anywhere = (pl.BlockSpec(memory_space=m) for m in (pltpu.VMEM, pl.ANY))
    buf = pltpu.VMEM
    dma = pltpu.SemaphoreType.DMA
    results = pl.pallas_call(
        functools.partial(kernel, ny, nz),
        out_shape=(
            jax.ShapeDtypeStruct((mine, width), BF16),
            jax.ShapeDtypeStruct((2, mine), F32),
            jax.ShapeDtypeStruct(weight_in.shape, BF16),
            jax.ShapeDtypeStruct(weight_out.shape, BF16),
        ),
        in_specs=[vmem, vmem] + [anywhere] * 4,
        out_specs=(vmem, vmem, anywhere, anywhere),
        scratch_shapes=[
            buf((tok, width), BF16),
            buf((tok, width), BF16),
            buf(weight_in.shape, BF16),
            buf(weight_out.shape, BF16),
            buf((2, 2, ny, 2, cap, width), BF16),
            buf((2, cap, tok), BF16),
            buf((units, 2, 4, 2, cap, 128), BF16),
            buf((units, 2, 2, 2, cap, 128), BF16),
            buf((units, 2, 2, cap, 128), BF16),
            buf((units, 2, 2, cap, 128), BF16),
            buf((2, 4, ny, 2, cap, 128), BF16),
            buf((2, 4, ny, 2, cap, 128), BF16),
            buf((units, 2, cap, width), BF16),
            buf((units, cap, width), BF16),
            buf((units, cap, width), BF16),
            buf((2, ny, cap, width), BF16),
            buf((8 * ny, 128), F32),
            buf((3, 8 * ny, 128), F32),
            buf((8 * ny, 128), F32),
            buf((8 * ny, 128), F32),
            buf((ny, 8, 128), F32),
            buf((ny, 8, 128), F32),
            buf((nz, mine, width), BF16),
            buf((nz, mine, width), BF16),
            buf((8, tok), F32),
            buf((nz, 8, tok), F32),
            buf(weight_in.shape, BF16),
            buf(weight_out.shape, BF16),
            dma((4,)),
            dma((2, 2)),
            dma,
            dma((2, ny)),
            dma,
            dma((2, ny)),
            dma,
            dma((units,)),
            dma,
            dma((units,)),
            dma,
            dma((units,)),
            dma,
            dma((units,)),
            dma,
            dma((2,)),
            dma,
            dma((2,)),
            dma,
            dma((units,)),
            dma,
            dma((2, ny)),
            dma,
            dma,
            dma,
            dma,
            dma,
            dma,
            dma,
            dma,
            dma,
            dma,
        ],
        compiler_params=pltpu.CompilerParams(
            collective_id=0, has_side_effects=True, vmem_limit_bytes=VMEM_BYTES
        ),
        name="expert_backward",
    )(routing.T, gate_prob.T, tokens, out_grad, weight_in, weight_out)
    gtok, ggate, gwi, gwo = pl.pallas_call(
        hand_over,
        out_shape=tuple(jax.ShapeDtypeStruct(r.shape, r.dtype) for r in results),
        in_specs=[anywhere] * 4,
        out_specs=(anywhere,) * 4,
        scratch_shapes=[buf(r.shape, r.dtype) for r in results] + [dma((2, 4))],
        compiler_params=pltpu.CompilerParams(vmem_limit_bytes=VMEM_BYTES),
        name="hand_over",
    )(*results)
    return gtok, ggate.T, gwi, gwo


def solution(mesh):
    ny, nz = mesh.shape["seq"] // 2, mesh.shape["exp"]
    return jax.shard_map(
        functools.partial(body, ny, nz),
        mesh=mesh,
        in_specs=(
            P("seq", "ffn"),
            P("seq", "ffn"),
            P("seq", None),
            P("seq", None),
            P("exp", "ffn", "seq"),
            P("exp", "seq", "ffn"),
        ),
        out_specs=(
            P(("seq", "exp"), "ffn"),
            P(("seq", "exp"), None),
            P("exp", "ffn", "seq"),
            P("exp", "seq", "ffn"),
        ),
        check_vma=False,
    )
```

```python
import functools

import jax
import jax.numpy as jnp
from jax import lax
from jax.experimental import pallas as pl
from jax.experimental.pallas import tpu as pltpu
from jax.sharding import PartitionSpec as P

MESH = pl.DeviceIdType.MESH
BF16, F32 = jnp.bfloat16, jnp.float32
gelu_scale = 0.7978845608028654
gelu_cubic = 0.044715
VMEM_BYTES = 62 * 2**20
LAGS = (2, 4, 6, 8, 9)
SECOND = 4


def gelu_parts(pre_act):
    square = pre_act * pre_act
    tangent = jnp.tanh(gelu_scale * pre_act * (1.0 + gelu_cubic * square))
    half = 0.5 * (1.0 + tangent)
    slope = half + 0.5 * pre_act * (1.0 - tangent * tangent) * gelu_scale * (
        1.0 + 3.0 * gelu_cubic * square
    )
    return pre_act * half, slope


def dot(a, b, over):
    return lax.dot_general(a, b, ((over[:1], over[1:]), ((), ())), preferred_element_type=F32)


def split(value):
    high = value.astype(BF16)
    return high, (value - high.astype(F32)).astype(BF16)


def kernel(
    ny, nz, route, gate, tok_h, og_h, win_h, wout_h,
    gtok, ggate, gwi_h, gwo_h,
    tok, og, win, wout, xy, sel, part, r1, r2, s1, act, dlt, bk, pb, ys, yr,
    g, gx, gs, gp, gt, gy, tb, zr, gz, gzr, gwi, gwo,
    in_sem, out_sem, ring_send, ring_recv, sib_send, sib_recv,
    r1_send, r1_recv, r2_send, r2_recv, d1_send, d1_recv, d2_send, d2_recv,
    a1_send, a1_recv, a2_send, a2_recv,
    pb_send, pb_recv, y_send, y_recv,
    gx_send, gx_recv, gp_send, gp_recv, gy_send, gy_recv, z_send, z_recv, gz_send, gz_recv,
):
    s, z, x = lax.axis_index("seq"), lax.axis_index("exp"), lax.axis_index("ffn")
    y, c = s // 2, s % 2
    sib = {"seq": s + 1 - 2 * c}
    xa, xb = {"ffn": x + 1 - 2 * (x % 2)}, {"ffn": 3 - x}
    h1, q1 = ((x + 1) // 2) % 2, x // 2
    h2, q2 = x // 2, x % 2
    units = 2 * ny
    cap = xy.shape[4]
    tokens = tok.shape[0]
    hid = win.shape[2]

    def along_y(step):
        return {"seq": ((y + step + ny) % ny) * 2 + c}

    def along_z(step):
        return {"exp": (z + step) % nz}

    def along_x(step):
        return {"ffn": (x + step) % 4}

    def send(src, dst, ssem, rsem, where):
        pltpu.make_async_remote_copy(
            src_ref=src, dst_ref=dst, send_sem=ssem, recv_sem=rsem,
            device_id=where, device_id_type=MESH,
        ).start()

    def done(ref, sem):
        pltpu.make_async_copy(ref, ref, sem).wait()

    loads = [
        pltpu.make_async_copy(a, b, in_sem.at[i])
        for i, (a, b) in enumerate(((tok_h, tok), (og_h, og), (win_h, win), (wout_h, wout)))
    ]
    for load in loads:
        load.start()

    barrier = pltpu.get_barrier_semaphore()
    peers = [sib]
    peers += [along_y(d) for d in range(1, ny)]
    peers += [along_x(d) for d in range(1, 4)]
    peers += [along_z(d) for d in range(1, nz)]
    for peer in peers:
        pl.semaphore_signal(barrier, inc=1, device_id=peer, device_id_type=MESH)

    def spread(e):
        reach = (ny // 2, ny // 2 - 1) if e == 0 else (ny // 2 - 1, ny // 2)
        own = xy.at[:, e, 0, c]
        if reach[0] > 0:
            send(own, xy.at[:, e, 1, c], ring_send, ring_recv.at[e, 1], along_y(-1))
        if reach[1] > 0:
            send(own, xy.at[:, e, ny - 1, c], ring_send, ring_recv.at[e, ny - 1], along_y(1))

    ids = [route[k : k + 1, :] for k in range(2)]
    probs = [gate[k : k + 1, :].astype(F32) for k in range(2)]
    named = [[r == 2 * z + e for r in ids] for e in range(2)]
    taken = [jnp.where(named[e][0] | named[e][1], 1.0, 0.0) for e in range(2)]
    weight = [
        jnp.where(named[e][0], probs[0], jnp.where(named[e][1], probs[1], 1.0)) for e in range(2)
    ]
    row_at = lax.broadcasted_iota(jnp.int32, (tokens, tokens), 0)
    col_at = lax.broadcasted_iota(jnp.int32, (tokens, tokens), 1)
    earlier = jnp.where(row_at < col_at, 1.0, 0.0).astype(BF16)
    slot_at = lax.broadcasted_iota(jnp.int32, (cap, tokens), 0).astype(F32)
    g[...] = jnp.zeros_like(g)
    loads[0].wait()
    loads[1].wait()
    for e in range(2):
        before = dot(jnp.broadcast_to(taken[e], (16, tokens)).astype(BF16), earlier, (1, 0))
        hit = (before[0:1, :] == slot_at) & (taken[e] > 0.5)
        sel[e] = jnp.where(hit, 1.0, 0.0).astype(BF16)
        scaled_sel = jnp.where(hit, weight[e], 0.0).astype(BF16)
        xy[0, e, 0, c] = dot(sel[e], tok[...], (1, 0)).astype(BF16)
        xy[1, e, 0, c] = dot(scaled_sel, og[...], (1, 0)).astype(BF16)
        if e == 0:
            pl.semaphore_wait(barrier, len(peers))
        own = xy.at[:, e, 0, c]
        send(own, own, sib_send, sib_recv.at[e, 0], sib)
        if e == 0:
            spread(0)
    loads[2].wait()
    loads[3].wait()

    def far(i):
        odd = i % 2
        return odd * ((i + 1) // 2) + (1 - odd) * ((ny - i // 2) % ny)

    def unit(u):
        own = 1 - jnp.minimum(u // 2, 1)
        late = jnp.minimum((u + own * ny) // (ny + 1), 1)
        e = own * u + (1 - own) * late
        v = u - ny - 1
        last = jnp.minimum((v + 3) // ny, 1) * late
        second = (1 - last) * (v + 3) + last * (ny - 1 - v)
        return e, far((1 - own) * ((1 - late) * (u - 1) + late * second))

    def pass_on(e, j):
        reach = (ny // 2, ny // 2 - 1) if e == 0 else (ny // 2 - 1, ny // 2)
        here = xy.at[:, e, j, c]
        done(here, ring_recv.at[e, j])
        send(here, here, sib_send, sib_recv.at[e, j], sib)

        @pl.when((j <= reach[0]) & (j < reach[0]))
        def _():
            send(here, xy.at[:, e, j + 1, c], ring_send, ring_recv.at[e, j + 1], along_y(-1))

        @pl.when((j >= ny - reach[1]) & (j > ny - reach[1]))
        def _():
            send(here, xy.at[:, e, j - 1, c], ring_send, ring_recv.at[e, j - 1], along_y(1))

    def products(u):
        e, j = unit(u)
        done(xy.at[:, e, j, 0], sib_recv.at[e, j])
        values = (
            dot(xy[0, e, j].reshape(2 * cap, -1), win[e], (1, 0)).astype(BF16),
            dot(xy[1, e, j].reshape(2 * cap, -1), wout[e], (1, 1)).astype(BF16),
        )
        for half in range(2):
            for b in range(4):
                for a in range(2):
                    part[u, half, b, a] = values[a][
                        half * cap : (half + 1) * cap, b * 128 : (b + 1) * 128
                    ]
        send(part.at[u, 0, pl.ds(2 * (1 - h1), 2)], r1.at[u, 0], r1_send, r1_recv.at[u], xa)
        send(part.at[u, 1, pl.ds(2 * (1 - h2), 2)], r1.at[u, 1], r1_send, r1_recv.at[u], xb)

    def halve(u):
        done(r1.at[u], r1_recv.at[u])
        for half, (h, q, to) in enumerate(((h1, q1, xb), (h2, q2, xa))):
            s1[u, half] = (
                part[u, half, 2 * h + 1 - q].astype(F32) + r1[u, half, 1 - q].astype(F32)
            ).astype(BF16)
            send(s1.at[u, half], r2.at[u, half], r2_send, r2_recv.at[u], to)

    def activate(u):
        e, j = unit(u)
        done(r2.at[u], r2_recv.at[u])
        terms = []
        for half, (h, q, to) in enumerate(((h1, q1, xb), (h2, q2, xa))):
            total = (
                part[u, half, 2 * h + q].astype(F32)
                + r1[u, half, q].astype(F32)
                + r2[u, half].astype(F32)
            )
            activated, slope = gelu_parts(total[0])
            act[e, 2 * h + q, j, half] = activated.astype(BF16)
            dlt[e, 2 * h + q, j, half] = (total[1] * slope).astype(BF16)
            piece = dlt.at[e, 2 * h + q, j, half]
            send(piece, piece, d1_send, d1_recv.at[u], to)
            terms.append(activated * total[1])
        high, low = split(jnp.concatenate(terms, axis=0))
        ones = jnp.ones((16, 2 * 128), BF16)
        summed = dot(ones, jnp.concatenate((high, low), axis=1), (1, 1))
        g[pl.ds(8 * j + e, 1), 0 : 2 * cap] = summed[0:1, :]

    def widen(u):
        e, j = unit(u)
        done(r2.at[u, 0], d1_recv.at[u])
        for half, (h, to) in enumerate(((h1, xa), (h2, xb))):
            piece = dlt.at[e, pl.ds(2 * h, 2), j, half]
            send(piece, piece, d2_send, d2_recv.at[u], to)

    def share_active(e):
        for half, (h, q, to) in enumerate(((h1, q1, xb), (h2, q2, xa))):
            piece = act.at[e, 2 * h + q, :, half]
            send(piece, piece, a1_send, a1_recv.at[e], to)

    def widen_active(e):
        done(act.at[e, 0], a1_recv.at[e])
        for half, (h, to) in enumerate(((h1, xa), (h2, xb))):
            piece = act.at[e, pl.ds(2 * h, 2), :, half]
            send(piece, piece, a2_send, a2_recv.at[e], to)

    def back(u):
        e, j = unit(u)
        done(r2.at[u], d2_recv.at[u])
        delta = jnp.concatenate(
            [dlt[e, b, j].reshape(2 * cap, 128) for b in range(4)], axis=1
        )
        bk[u] = dot(delta, win[e], (1, 1)).astype(BF16).reshape(2, cap, -1)
        send(bk.at[u, 1 - c], pb.at[u], pb_send, pb_recv.at[u], sib)

    def deliver(u):
        e, j = unit(u)
        done(pb.at[u], pb_recv.at[u])
        both = (bk[u, c].astype(F32) + pb[u].astype(F32)).astype(BF16)

        @pl.when(j == 0)
        def _():
            yr[e, 0] = both

        @pl.when(j > 0)
        def _():
            ys[u] = both
            send(ys.at[u], yr.at[e, j], y_send, y_recv.at[e, j], along_y(j))

    def two_blocks(ref, e, p):
        return jnp.concatenate(
            [ref[e, 2 * p + b].reshape(2 * ny * cap, 128) for b in range(2)], axis=1
        )

    def grad_in(e, p):
        values = xy[0, e].reshape(2 * ny * cap, -1)
        cols = pl.ds(p * (hid // 2), hid // 2)
        gwi[e, :, cols] = dot(values, two_blocks(dlt, e, p), (0, 0)).astype(BF16)

    def grad_out(e, p):
        values = xy[1, e].reshape(2 * ny * cap, -1)
        rows = pl.ds(p * (hid // 2), hid // 2)
        gwo[e, rows, :] = dot(two_blocks(act, e, p), values, (0, 0)).astype(BF16)

    def store_in(e):
        return pltpu.make_async_copy(gwi.at[e], gwi_h.at[e], out_sem.at[e, 0])

    def store_out(e):
        return pltpu.make_async_copy(gwo.at[e], gwo_h.at[e], out_sem.at[e, 1])

    def step(k, carry):
        def stage(lag, work):
            @pl.when((k >= lag) & (k < units + lag))
            def _():
                work(k - lag)

        stage(0, products)
        stage(LAGS[0], halve)
        stage(LAGS[1], activate)
        stage(LAGS[2], widen)

        @pl.when((k > 0) & (k < ny))
        def _():
            pass_on(0, far(k))

        @pl.when(k == SECOND)
        def _():
            spread(1)

        @pl.when((k > SECOND) & (k < SECOND + ny))
        def _():
            pass_on(1, far(k - SECOND))

        stage(LAGS[3], back)
        stage(LAGS[4], deliver)

        @pl.when(k == units - 1 + LAGS[1])
        def _():
            for d in range(1, 4):
                send(g, gx.at[d - 1], gx_send, gx_recv, along_x(d))

        @pl.when(k == units - 1 + LAGS[2])
        def _():
            done(gx, gx_recv)
            gs[...] = g[...] + gx[0] + gx[1] + gx[2]
            send(gs, gp, gp_send, gp_recv, sib)

        @pl.when(k == units - 1 + LAGS[3])
        def _():
            done(gp, gp_recv)
            gt[...] = (gs[...] + gp[...]).reshape(gt.shape)
            gy[0] = gt[0]
            for d in range(1, ny):
                send(gt.at[d], gy.at[d], gy_send, gy_recv, along_y(d))

        @pl.when(k == units - 1 + LAGS[1])
        def _():
            share_active(0)

        @pl.when(k == units - 1 + LAGS[2])
        def _():
            share_active(1)

        for p in range(2):
            @pl.when(k == ny + 1 + LAGS[3] + p)
            def _():
                grad_in(0, p)

        @pl.when(k == ny + 3 + LAGS[3])
        def _():
            store_in(0).start()

        return carry

    lax.fori_loop(0, units + LAGS[4], step, 0)
    widen_active(0)
    widen_active(1)

    rows = []
    for e in range(2):
        for j in range(1, ny):
            done(yr.at[e, j], y_recv.at[e, j])
        rows.append(jnp.sum(yr[e].astype(F32), axis=0).astype(BF16))
    for e in range(2):
        own = dot(sel[e], rows[e], (0, 0))
        total = own if e == 0 else total + own
    tb[...] = total.astype(BF16).reshape(tb.shape)
    for d in range(1, nz):
        send(tb.at[(z + d) % nz], zr.at[d], z_send, z_recv, along_z(d))

    done(gy.at[pl.ds(1, ny - 1)], gy_recv)
    term = jnp.sum(gy[...], axis=0)
    term = jnp.where(c == 0, term[:, 0:cap], term[:, cap : 2 * cap])
    term = jnp.concatenate((term, jnp.zeros_like(term)), axis=0)
    high, low = split(term)
    at_token = []
    for e in range(2):
        value = dot(high, sel[e], (1, 0)) + dot(low, sel[e], (1, 0))
        at_token.append(value[e : e + 1, :] / weight[e])
    gz[...] = jnp.zeros_like(gz)
    for k in range(2):
        gz[k : k + 1, :] = jnp.where(named[0][k], at_token[0], 0.0) + jnp.where(
            named[1][k], at_token[1], 0.0
        )
    for d in range(1, nz):
        send(gz, gzr.at[d], gz_send, gz_recv, along_z(d))

    for p in range(2):
        grad_in(1, p)
    store_in(1).start()

    def finish_out(e):
        done(act.at[e, pl.ds(0, 2)], a2_recv.at[e])
        for p in range(2):
            grad_out(e, p)
        store_out(e).start()

    finish_out(0)
    out = tb[z].astype(F32)
    gates = gz[...]
    if nz > 1:
        done(zr.at[pl.ds(1, nz - 1)], z_recv)
        done(gzr.at[pl.ds(1, nz - 1)], gz_recv)
        for d in range(1, nz):
            out = out + zr[d].astype(F32)
            gates = gates + gzr[d]
    gtok[...] = out.astype(BF16)
    mine = gtok.shape[0]
    pick = jnp.where(
        lax.broadcasted_iota(jnp.int32, (mine, tokens), 1)
        == lax.broadcasted_iota(jnp.int32, (mine, tokens), 0) + z * mine,
        1.0,
        0.0,
    ).astype(BF16)
    high, low = split(jnp.concatenate((gates, jnp.zeros_like(gates)), axis=0))
    ggate[...] = (dot(high, pick, (1, 1)) + dot(low, pick, (1, 1)))[0:2, :]

    finish_out(1)

    done(xy.at[:, :, pl.ds(0, ny - 1), 0], ring_send)
    done(xy.at[:, :, :, 0], sib_send)
    done(r1, r1_send)
    done(r2, r2_send)
    done(r2.at[:, 0], d1_send)
    done(r2, d2_send)
    done(act.at[:, 0], a1_send)
    done(act.at[:, pl.ds(0, 2)], a2_send)
    done(pb, pb_send)
    done(ys.at[pl.ds(0, 2 * (ny - 1))], y_send)
    done(gx, gx_send)
    done(gp, gp_send)
    done(gy.at[pl.ds(1, ny - 1)], gy_send)
    if nz > 1:
        done(zr.at[pl.ds(1, nz - 1)], z_send)
        done(gzr.at[pl.ds(1, nz - 1)], gz_send)
    for e in range(2):
        store_in(e).wait()
        store_out(e).wait()


def hand_over(*refs):
    given, out, held, sems = refs[:4], refs[4:8], refs[8:12], refs[12]
    loads = [pltpu.make_async_copy(given[i], held[i], sems.at[0, i]) for i in range(4)]
    stores = [pltpu.make_async_copy(held[i], out[i], sems.at[1, i]) for i in range(4)]
    for load in loads:
        load.start()
    for load, store in zip(loads, stores):
        load.wait()
        store.start()
    for store in stores:
        store.wait()


def body(ny, nz, tokens, out_grad, gate_prob, routing, weight_in, weight_out):
    tok, width = tokens.shape
    hid = weight_in.shape[2]
    cap = 3 * tok // (2 * nz)
    units = 2 * ny
    mine = tok // nz
    vmem, anywhere = (pl.BlockSpec(memory_space=m) for m in (pltpu.VMEM, pl.ANY))
    buf = pltpu.VMEM
    dma = pltpu.SemaphoreType.DMA
    results = pl.pallas_call(
        functools.partial(kernel, ny, nz),
        out_shape=(
            jax.ShapeDtypeStruct((mine, width), BF16),
            jax.ShapeDtypeStruct((2, mine), F32),
            jax.ShapeDtypeStruct(weight_in.shape, BF16),
            jax.ShapeDtypeStruct(weight_out.shape, BF16),
        ),
        in_specs=[vmem, vmem] + [anywhere] * 4,
        out_specs=(vmem, vmem, anywhere, anywhere),
        scratch_shapes=[
            buf((tok, width), BF16),
            buf((tok, width), BF16),
            buf(weight_in.shape, BF16),
            buf(weight_out.shape, BF16),
            buf((2, 2, ny, 2, cap, width), BF16),
            buf((2, cap, tok), BF16),
            buf((units, 2, 4, 2, cap, 128), BF16),
            buf((units, 2, 2, 2, cap, 128), BF16),
            buf((units, 2, 2, cap, 128), BF16),
            buf((units, 2, 2, cap, 128), BF16),
            buf((2, 4, ny, 2, cap, 128), BF16),
            buf((2, 4, ny, 2, cap, 128), BF16),
            buf((units, 2, cap, width), BF16),
            buf((units, cap, width), BF16),
            buf((units, cap, width), BF16),
            buf((2, ny, cap, width), BF16),
            buf((8 * ny, 128), F32),
            buf((3, 8 * ny, 128), F32),
            buf((8 * ny, 128), F32),
            buf((8 * ny, 128), F32),
            buf((ny, 8, 128), F32),
            buf((ny, 8, 128), F32),
            buf((nz, mine, width), BF16),
            buf((nz, mine, width), BF16),
            buf((8, tok), F32),
            buf((nz, 8, tok), F32),
            buf(weight_in.shape, BF16),
            buf(weight_out.shape, BF16),
            dma((4,)),
            dma((2, 2)),
            dma,
            dma((2, ny)),
            dma,
            dma((2, ny)),
            dma,
            dma((units,)),
            dma,
            dma((units,)),
            dma,
            dma((units,)),
            dma,
            dma((units,)),
            dma,
            dma((2,)),
            dma,
            dma((2,)),
            dma,
            dma((units,)),
            dma,
            dma((2, ny)),
            dma,
            dma,
            dma,
            dma,
            dma,
            dma,
            dma,
            dma,
            dma,
            dma,
        ],
        compiler_params=pltpu.CompilerParams(
            collective_id=0, has_side_effects=True, vmem_limit_bytes=VMEM_BYTES
        ),
        name="expert_backward",
    )(routing.T, gate_prob.T, tokens, out_grad, weight_in, weight_out)
    gtok, ggate, gwi, gwo = pl.pallas_call(
        hand_over,
        out_shape=tuple(jax.ShapeDtypeStruct(r.shape, r.dtype) for r in results),
        in_specs=[anywhere] * 4,
        out_specs=(anywhere,) * 4,
        scratch_shapes=[buf(r.shape, r.dtype) for r in results] + [dma((2, 4))],
        compiler_params=pltpu.CompilerParams(vmem_limit_bytes=VMEM_BYTES),
        name="hand_over",
    )(*results)
    return gtok, ggate.T, gwi, gwo


def solution(mesh):
    ny, nz = mesh.shape["seq"] // 2, mesh.shape["exp"]
    return jax.shard_map(
        functools.partial(body, ny, nz),
        mesh=mesh,
        in_specs=(
            P("seq", "ffn"),
            P("seq", "ffn"),
            P("seq", None),
            P("seq", None),
            P("exp", "ffn", "seq"),
            P("exp", "seq", "ffn"),
        ),
        out_specs=(
            P(("seq", "exp"), "ffn"),
            P(("seq", "exp"), None),
            P("exp", "ffn", "seq"),
            P("exp", "seq", "ffn"),
        ),
        check_vma=False,
    )
```

```python
import functools

import jax
import jax.numpy as jnp
from jax import lax
from jax.experimental import pallas as pl
from jax.experimental.pallas import tpu as pltpu
from jax.sharding import PartitionSpec as P

MESH = pl.DeviceIdType.MESH
BF16, F32 = jnp.bfloat16, jnp.float32
gelu_scale = 0.7978845608028654
gelu_cubic = 0.044715
VMEM_BYTES = 62 * 2**20
LAGS = (2, 4, 6, 8, 9)
SECOND = 4


def gelu_parts(pre_act):
    square = pre_act * pre_act
    tangent = jnp.tanh(gelu_scale * pre_act * (1.0 + gelu_cubic * square))
    half = 0.5 * (1.0 + tangent)
    slope = half + 0.5 * pre_act * (1.0 - tangent * tangent) * gelu_scale * (
        1.0 + 3.0 * gelu_cubic * square
    )
    return pre_act * half, slope


def dot(a, b, over):
    return lax.dot_general(a, b, ((over[:1], over[1:]), ((), ())), preferred_element_type=F32)


def split(value):
    high = value.astype(BF16)
    return high, (value - high.astype(F32)).astype(BF16)


def kernel(
    ny, nz, route, gate, tok_h, og_h, win_h, wout_h,
    gtok, ggate, gwi_h, gwo_h,
    tok, og, win, wout, xy, sel, part, r1, r2, s1, act, dlt, bk, pb, ys, yr,
    g, gx, gs, gp, gt, gy, tb, zr, gz, gzr, gwi, gwo,
    in_sem, out_sem, ring_send, ring_recv, sib_send, sib_recv,
    r1_send, r1_recv, r2_send, r2_recv, d1_send, d1_recv, d2_send, d2_recv,
    a1_send, a1_recv, a2_send, a2_recv,
    pb_send, pb_recv, y_send, y_recv,
    gx_send, gx_recv, gp_send, gp_recv, gy_send, gy_recv, z_send, z_recv, gz_send, gz_recv,
):
    s, z, x = lax.axis_index("seq"), lax.axis_index("exp"), lax.axis_index("ffn")
    y, c = s // 2, s % 2
    sib = {"seq": s + 1 - 2 * c}
    xa, xb = {"ffn": x + 1 - 2 * (x % 2)}, {"ffn": 3 - x}
    h1, q1 = ((x + 1) // 2) % 2, x // 2
    h2, q2 = x // 2, x % 2
    units = 2 * ny
    cap = xy.shape[4]
    tokens = tok.shape[0]
    hid = win.shape[2]

    def along_y(step):
        return {"seq": ((y + step + ny) % ny) * 2 + c}

    def along_z(step):
        return {"exp": (z + step) % nz}

    def along_x(step):
        return {"ffn": (x + step) % 4}

    def send(src, dst, ssem, rsem, where):
        pltpu.make_async_remote_copy(
            src_ref=src, dst_ref=dst, send_sem=ssem, recv_sem=rsem,
            device_id=where, device_id_type=MESH,
        ).start()

    def done(ref, sem):
        pltpu.make_async_copy(ref, ref, sem).wait()

    loads = [
        pltpu.make_async_copy(a, b, in_sem.at[i])
        for i, (a, b) in enumerate(((tok_h, tok), (og_h, og), (win_h, win), (wout_h, wout)))
    ]
    for load in loads:
        load.start()

    barrier = pltpu.get_barrier_semaphore()
    peers = [sib]
    peers += [along_y(d) for d in range(1, ny)]
    peers += [along_x(d) for d in range(1, 4)]
    peers += [along_z(d) for d in range(1, nz)]
    for peer in peers:
        pl.semaphore_signal(barrier, inc=1, device_id=peer, device_id_type=MESH)

    def spread(e):
        reach = (ny // 2, ny // 2 - 1) if e == 0 else (ny // 2 - 1, ny // 2)
        own = xy.at[:, e, 0, c]
        if reach[0] > 0:
            send(own, xy.at[:, e, 1, c], ring_send, ring_recv.at[e, 1], along_y(-1))
        if reach[1] > 0:
            send(own, xy.at[:, e, ny - 1, c], ring_send, ring_recv.at[e, ny - 1], along_y(1))

    ids = [route[k : k + 1, :] for k in range(2)]
    probs = [gate[k : k + 1, :].astype(F32) for k in range(2)]
    named = [[r == 2 * z + e for r in ids] for e in range(2)]
    taken = [jnp.where(named[e][0] | named[e][1], 1.0, 0.0) for e in range(2)]
    weight = [
        jnp.where(named[e][0], probs[0], jnp.where(named[e][1], probs[1], 1.0)) for e in range(2)
    ]
    row_at = lax.broadcasted_iota(jnp.int32, (tokens, tokens), 0)
    col_at = lax.broadcasted_iota(jnp.int32, (tokens, tokens), 1)
    earlier = jnp.where(row_at < col_at, 1.0, 0.0).astype(BF16)
    slot_at = lax.broadcasted_iota(jnp.int32, (cap, tokens), 0).astype(F32)
    g[...] = jnp.zeros_like(g)
    loads[0].wait()
    loads[1].wait()
    for e in range(2):
        before = dot(jnp.broadcast_to(taken[e], (16, tokens)).astype(BF16), earlier, (1, 0))
        hit = (before[0:1, :] == slot_at) & (taken[e] > 0.5)
        sel[e] = jnp.where(hit, 1.0, 0.0).astype(BF16)
        scaled_sel = jnp.where(hit, weight[e], 0.0).astype(BF16)
        xy[0, e, 0, c] = dot(sel[e], tok[...], (1, 0)).astype(BF16)
        xy[1, e, 0, c] = dot(scaled_sel, og[...], (1, 0)).astype(BF16)
        if e == 0:
            pl.semaphore_wait(barrier, len(peers))
        own = xy.at[:, e, 0, c]
        send(own, own, sib_send, sib_recv.at[e, 0], sib)
        if e == 0:
            spread(0)
    loads[2].wait()
    loads[3].wait()

    def far(i):
        odd = i % 2
        return odd * ((i + 1) // 2) + (1 - odd) * ((ny - i // 2) % ny)

    def unit(u):
        own = 1 - jnp.minimum(u // 2, 1)
        late = jnp.minimum((u + own * ny) // (ny + 1), 1)
        e = own * u + (1 - own) * late
        v = u - ny - 1
        last = jnp.minimum((v + 3) // ny, 1) * late
        second = (1 - last) * (v + 3) + last * (ny - 1 - v)
        return e, far((1 - own) * ((1 - late) * (u - 1) + late * second))

    def pass_on(e, j):
        reach = (ny // 2, ny // 2 - 1) if e == 0 else (ny // 2 - 1, ny // 2)
        here = xy.at[:, e, j, c]
        done(here, ring_recv.at[e, j])
        send(here, here, sib_send, sib_recv.at[e, j], sib)

        @pl.when((j <= reach[0]) & (j < reach[0]))
        def _():
            send(here, xy.at[:, e, j + 1, c], ring_send, ring_recv.at[e, j + 1], along_y(-1))

        @pl.when((j >= ny - reach[1]) & (j > ny - reach[1]))
        def _():
            send(here, xy.at[:, e, j - 1, c], ring_send, ring_recv.at[e, j - 1], along_y(1))

    def products(u):
        e, j = unit(u)
        done(xy.at[:, e, j, 0], sib_recv.at[e, j])
        values = (
            dot(xy[0, e, j].reshape(2 * cap, -1), win[e], (1, 0)).astype(BF16),
            dot(xy[1, e, j].reshape(2 * cap, -1), wout[e], (1, 1)).astype(BF16),
        )
        for half in range(2):
            for b in range(4):
                for a in range(2):
                    part[u, half, b, a] = values[a][
                        half * cap : (half + 1) * cap, b * 128 : (b + 1) * 128
                    ]
        send(part.at[u, 0, pl.ds(2 * (1 - h1), 2)], r1.at[u, 0], r1_send, r1_recv.at[u], xa)
        send(part.at[u, 1, pl.ds(2 * (1 - h2), 2)], r1.at[u, 1], r1_send, r1_recv.at[u], xb)

    def halve(u):
        done(r1.at[u], r1_recv.at[u])
        for half, (h, q, to) in enumerate(((h1, q1, xb), (h2, q2, xa))):
            s1[u, half] = (
                part[u, half, 2 * h + 1 - q].astype(F32) + r1[u, half, 1 - q].astype(F32)
            ).astype(BF16)
            send(s1.at[u, half], r2.at[u, half], r2_send, r2_recv.at[u], to)

    def activate(u):
        e, j = unit(u)
        done(r2.at[u], r2_recv.at[u])
        terms = []
        for half, (h, q, to) in enumerate(((h1, q1, xb), (h2, q2, xa))):
            total = (
                part[u, half, 2 * h + q].astype(F32)
                + r1[u, half, q].astype(F32)
                + r2[u, half].astype(F32)
            )
            activated, slope = gelu_parts(total[0])
            act[e, 2 * h + q, j, half] = activated.astype(BF16)
            dlt[e, 2 * h + q, j, half] = (total[1] * slope).astype(BF16)
            piece = dlt.at[e, 2 * h + q, j, half]
            send(piece, piece, d1_send, d1_recv.at[u], to)
            terms.append(activated * total[1])
        high, low = split(jnp.concatenate(terms, axis=0))
        ones = jnp.ones((16, 2 * 128), BF16)
        summed = dot(ones, jnp.concatenate((high, low), axis=1), (1, 1))
        g[pl.ds(8 * j + e, 1), 0 : 2 * cap] = summed[0:1, :]

    def widen(u):
        e, j = unit(u)
        done(r2.at[u, 0], d1_recv.at[u])
        for half, (h, to) in enumerate(((h1, xa), (h2, xb))):
            piece = dlt.at[e, pl.ds(2 * h, 2), j, half]
            send(piece, piece, d2_send, d2_recv.at[u], to)

    def share_active(e):
        for half, (h, q, to) in enumerate(((h1, q1, xb), (h2, q2, xa))):
            piece = act.at[e, 2 * h + q, :, half]
            send(piece, piece, a1_send, a1_recv.at[e], to)

    def widen_active(e):
        done(act.at[e, 0], a1_recv.at[e])
        for half, (h, to) in enumerate(((h1, xa), (h2, xb))):
            piece = act.at[e, pl.ds(2 * h, 2), :, half]
            send(piece, piece, a2_send, a2_recv.at[e], to)

    def back(u):
        e, j = unit(u)
        done(r2.at[u], d2_recv.at[u])
        delta = jnp.concatenate(
            [dlt[e, b, j].reshape(2 * cap, 128) for b in range(4)], axis=1
        )
        bk[u] = dot(delta, win[e], (1, 1)).astype(BF16).reshape(2, cap, -1)
        send(bk.at[u, 1 - c], pb.at[u], pb_send, pb_recv.at[u], sib)

    def deliver(u):
        e, j = unit(u)
        done(pb.at[u], pb_recv.at[u])
        both = (bk[u, c].astype(F32) + pb[u].astype(F32)).astype(BF16)

        @pl.when(j == 0)
        def _():
            yr[e, 0] = both

        @pl.when(j > 0)
        def _():
            ys[u] = both
            send(ys.at[u], yr.at[e, j], y_send, y_recv.at[e, j], along_y(j))

    def two_blocks(ref, e, p):
        return jnp.concatenate(
            [ref[e, 2 * p + b].reshape(2 * ny * cap, 128) for b in range(2)], axis=1
        )

    def grad_in(e, p):
        values = xy[0, e].reshape(2 * ny * cap, -1)
        cols = pl.ds(p * (hid // 2), hid // 2)
        gwi[e, :, cols] = dot(values, two_blocks(dlt, e, p), (0, 0)).astype(BF16)

    def grad_out(e, p):
        values = xy[1, e].reshape(2 * ny * cap, -1)
        rows = pl.ds(p * (hid // 2), hid // 2)
        gwo[e, rows, :] = dot(two_blocks(act, e, p), values, (0, 0)).astype(BF16)

    def store_in(e):
        return pltpu.make_async_copy(gwi.at[e], gwi_h.at[e], out_sem.at[e, 0])

    def store_out(e):
        return pltpu.make_async_copy(gwo.at[e], gwo_h.at[e], out_sem.at[e, 1])

    def step(k, carry):
        def stage(lag, work):
            @pl.when((k >= lag) & (k < units + lag))
            def _():
                work(k - lag)

        stage(0, products)
        stage(LAGS[0], halve)
        stage(LAGS[1], activate)
        stage(LAGS[2], widen)

        @pl.when((k > 0) & (k < ny))
        def _():
            pass_on(0, far(k))

        @pl.when(k == SECOND)
        def _():
            spread(1)

        @pl.when((k > SECOND) & (k < SECOND + ny))
        def _():
            pass_on(1, far(k - SECOND))

        stage(LAGS[3], back)
        stage(LAGS[4], deliver)

        @pl.when(k == units - 1 + LAGS[1])
        def _():
            for d in range(1, 4):
                send(g, gx.at[d - 1], gx_send, gx_recv, along_x(d))

        @pl.when(k == units - 1 + LAGS[2])
        def _():
            done(gx, gx_recv)
            gs[...] = g[...] + gx[0] + gx[1] + gx[2]
            send(gs, gp, gp_send, gp_recv, sib)

        @pl.when(k == units - 1 + LAGS[3])
        def _():
            done(gp, gp_recv)
            gt[...] = (gs[...] + gp[...]).reshape(gt.shape)
            gy[0] = gt[0]
            for d in range(1, ny):
                send(gt.at[d], gy.at[d], gy_send, gy_recv, along_y(d))

        @pl.when(k == units - 1 + LAGS[1])
        def _():
            share_active(0)

        @pl.when(k == units - 1 + LAGS[2])
        def _():
            share_active(1)

        for p in range(2):
            @pl.when(k == ny + 1 + LAGS[3] + p)
            def _():
                grad_in(0, p)

        @pl.when(k == ny + 3 + LAGS[3])
        def _():
            store_in(0).start()

        return carry

    lax.fori_loop(0, units + LAGS[4], step, 0)
    widen_active(0)
    widen_active(1)

    rows = []
    for e in range(2):
        for j in range(1, ny):
            done(yr.at[e, j], y_recv.at[e, j])
        rows.append(jnp.sum(yr[e].astype(F32), axis=0).astype(BF16))
    for e in range(2):
        own = dot(sel[e], rows[e], (0, 0))
        total = own if e == 0 else total + own
    tb[...] = total.astype(BF16).reshape(tb.shape)
    for d in sorted(range(1, nz), key=lambda d: -min(d, nz - d)):
        send(tb.at[(z + d) % nz], zr.at[d], z_send, z_recv, along_z(d))

    done(gy.at[pl.ds(1, ny - 1)], gy_recv)
    term = jnp.sum(gy[...], axis=0)
    term = jnp.where(c == 0, term[:, 0:cap], term[:, cap : 2 * cap])
    term = jnp.concatenate((term, jnp.zeros_like(term)), axis=0)
    high, low = split(term)
    at_token = []
    for e in range(2):
        value = dot(high, sel[e], (1, 0)) + dot(low, sel[e], (1, 0))
        at_token.append(value[e : e + 1, :] / weight[e])
    gz[...] = jnp.zeros_like(gz)
    for k in range(2):
        gz[k : k + 1, :] = jnp.where(named[0][k], at_token[0], 0.0) + jnp.where(
            named[1][k], at_token[1], 0.0
        )
    for d in range(1, nz):
        send(gz, gzr.at[d], gz_send, gz_recv, along_z(d))

    for p in range(2):
        grad_in(1, p)
    store_in(1).start()

    def finish_out(e):
        done(act.at[e, pl.ds(0, 2)], a2_recv.at[e])
        for p in range(2):
            grad_out(e, p)
        store_out(e).start()

    finish_out(0)
    finish_out(1)
    out = tb[z].astype(F32)
    gates = gz[...]
    if nz > 1:
        done(zr.at[pl.ds(1, nz - 1)], z_recv)
        done(gzr.at[pl.ds(1, nz - 1)], gz_recv)
        for d in range(1, nz):
            out = out + zr[d].astype(F32)
            gates = gates + gzr[d]
    gtok[...] = out.astype(BF16)
    mine = gtok.shape[0]
    pick = jnp.where(
        lax.broadcasted_iota(jnp.int32, (mine, tokens), 1)
        == lax.broadcasted_iota(jnp.int32, (mine, tokens), 0) + z * mine,
        1.0,
        0.0,
    ).astype(BF16)
    high, low = split(jnp.concatenate((gates, jnp.zeros_like(gates)), axis=0))
    ggate[...] = (dot(high, pick, (1, 1)) + dot(low, pick, (1, 1)))[0:2, :]

    done(xy.at[:, :, pl.ds(0, ny - 1), 0], ring_send)
    done(xy.at[:, :, :, 0], sib_send)
    done(r1, r1_send)
    done(r2, r2_send)
    done(r2.at[:, 0], d1_send)
    done(r2, d2_send)
    done(act.at[:, 0], a1_send)
    done(act.at[:, pl.ds(0, 2)], a2_send)
    done(pb, pb_send)
    done(ys.at[pl.ds(0, 2 * (ny - 1))], y_send)
    done(gx, gx_send)
    done(gp, gp_send)
    done(gy.at[pl.ds(1, ny - 1)], gy_send)
    if nz > 1:
        done(zr.at[pl.ds(1, nz - 1)], z_send)
        done(gzr.at[pl.ds(1, nz - 1)], gz_send)
    for e in range(2):
        store_in(e).wait()
        store_out(e).wait()


def hand_over(*refs):
    given, out, held, sems = refs[:4], refs[4:8], refs[8:12], refs[12]
    pieces = [(2, 0), (3, 0), (2, 1), (3, 1), (0, None), (1, None)]
    loads, stores = [], []
    for n, (i, e) in enumerate(pieces):
        a, b, d = (r[i] if e is None else r[i].at[e] for r in (given, held, out))
        loads.append(pltpu.make_async_copy(a, b, sems.at[0, n]))
        stores.append(pltpu.make_async_copy(b, d, sems.at[1, n]))
    for load in loads:
        load.start()
    for load, store in zip(loads, stores):
        load.wait()
        store.start()
    for store in stores:
        store.wait()


def body(ny, nz, tokens, out_grad, gate_prob, routing, weight_in, weight_out):
    tok, width = tokens.shape
    hid = weight_in.shape[2]
    cap = 3 * tok // (2 * nz)
    units = 2 * ny
    mine = tok // nz
    vmem, anywhere = (pl.BlockSpec(memory_space=m) for m in (pltpu.VMEM, pl.ANY))
    buf = pltpu.VMEM
    dma = pltpu.SemaphoreType.DMA
    results = pl.pallas_call(
        functools.partial(kernel, ny, nz),
        out_shape=(
            jax.ShapeDtypeStruct((mine, width), BF16),
            jax.ShapeDtypeStruct((2, mine), F32),
            jax.ShapeDtypeStruct(weight_in.shape, BF16),
            jax.ShapeDtypeStruct(weight_out.shape, BF16),
        ),
        in_specs=[vmem, vmem] + [anywhere] * 4,
        out_specs=(vmem, vmem, anywhere, anywhere),
        scratch_shapes=[
            buf((tok, width), BF16),
            buf((tok, width), BF16),
            buf(weight_in.shape, BF16),
            buf(weight_out.shape, BF16),
            buf((2, 2, ny, 2, cap, width), BF16),
            buf((2, cap, tok), BF16),
            buf((units, 2, 4, 2, cap, 128), BF16),
            buf((units, 2, 2, 2, cap, 128), BF16),
            buf((units, 2, 2, cap, 128), BF16),
            buf((units, 2, 2, cap, 128), BF16),
            buf((2, 4, ny, 2, cap, 128), BF16),
            buf((2, 4, ny, 2, cap, 128), BF16),
            buf((units, 2, cap, width), BF16),
            buf((units, cap, width), BF16),
            buf((units, cap, width), BF16),
            buf((2, ny, cap, width), BF16),
            buf((8 * ny, 128), F32),
            buf((3, 8 * ny, 128), F32),
            buf((8 * ny, 128), F32),
            buf((8 * ny, 128), F32),
            buf((ny, 8, 128), F32),
            buf((ny, 8, 128), F32),
            buf((nz, mine, width), BF16),
            buf((nz, mine, width), BF16),
            buf((8, tok), F32),
            buf((nz, 8, tok), F32),
            buf(weight_in.shape, BF16),
            buf(weight_out.shape, BF16),
            dma((4,)),
            dma((2, 2)),
            dma,
            dma((2, ny)),
            dma,
            dma((2, ny)),
            dma,
            dma((units,)),
            dma,
            dma((units,)),
            dma,
            dma((units,)),
            dma,
            dma((units,)),
            dma,
            dma((2,)),
            dma,
            dma((2,)),
            dma,
            dma((units,)),
            dma,
            dma((2, ny)),
            dma,
            dma,
            dma,
            dma,
            dma,
            dma,
            dma,
            dma,
            dma,
            dma,
        ],
        compiler_params=pltpu.CompilerParams(
            collective_id=0, has_side_effects=True, vmem_limit_bytes=VMEM_BYTES
        ),
        name="expert_backward",
    )(routing.T, gate_prob.T, tokens, out_grad, weight_in, weight_out)
    gtok, ggate, gwi, gwo = pl.pallas_call(
        hand_over,
        out_shape=tuple(jax.ShapeDtypeStruct(r.shape, r.dtype) for r in results),
        in_specs=[anywhere] * 4,
        out_specs=(anywhere,) * 4,
        scratch_shapes=[buf(r.shape, r.dtype) for r in results] + [dma((2, 6))],
        compiler_params=pltpu.CompilerParams(vmem_limit_bytes=VMEM_BYTES),
        name="hand_over",
    )(*results)
    return gtok, ggate.T, gwi, gwo


def solution(mesh):
    ny, nz = mesh.shape["seq"] // 2, mesh.shape["exp"]
    return jax.shard_map(
        functools.partial(body, ny, nz),
        mesh=mesh,
        in_specs=(
            P("seq", "ffn"),
            P("seq", "ffn"),
            P("seq", None),
            P("seq", None),
            P("exp", "ffn", "seq"),
            P("exp", "seq", "ffn"),
        ),
        out_specs=(
            P(("seq", "exp"), "ffn"),
            P(("seq", "exp"), None),
            P("exp", "ffn", "seq"),
            P("exp", "seq", "ffn"),
        ),
        check_vma=False,
    )
```
